256 devices in a mesh: inst: 8 (over x_hi, y), slab: 32 (over z, x_lo, core).
Axes of the slice: x: 4 (x_hi: 2, x_lo: 2; x = x_hi * 2 + x_lo), y: 4, z: 8, core: 2. Of those that a mesh axis runs over, the one named last changes fastest.
Arguments:
- volume_frac: float32 [8, 256, 64, 512], P('inst', 'slab'), may hold values from 0 to 1
- velocity_u: float32 [8, 256, 64, 512], P('inst', 'slab'), may hold values from -6 to 6
- velocity_v: float32 [8, 256, 64, 512], P('inst', 'slab'), may hold values from -6 to 6
- velocity_w: float32 [8, 256, 64, 512], P('inst', 'slab'), may hold values from -6 to 6
- wetted: int32 [8, 256, 64, 512], P('inst', 'slab'), may hold values 0 or 1
- section_map: int32 [256, 64, 512], P('slab'), may hold values from 0 to 63, as said below
Outputs:
- residual: float32 [8, 256, 64, 512], P('inst', 'slab')
- section_loads: float32 [8, 2, 64], P('inst', None, 'slab')
The draws below stay inside these ranges and needn't reach their ends.
Inputs may be any that keep to these rules, and one draw needn't show every extreme that they name: `section_map`: a cell in longitudinal column x maps to a section within one of x * 64 // 512.
All inputs are finite; a program needn't handle non-finite values. No bound on the sum of `wetted` on one device may be relied on, other than what follows from the above.
Results may differ from the reference program's by a relative error of at most 0.00022.
Values sent between devices are 32-bit elements; how exact they have to be, the bound alone decides.
A program may use at most 64 MiB of HBM per device.

```python
import jax
import jax.numpy as jnp
from jax import lax

CV = 8
NY = 64
NX = 512
SEC_DEV = 2
INSTANCES = 8
NV = 256
NSEC = 64


def draw_section_map(key, part):
    base = jnp.arange(NX, dtype=jnp.int32) * NSEC // NX
    jitter = jax.random.randint(key, (NV, NY, NX), -1, 2, dtype=jnp.int32)
    return jnp.clip(base[None, None, :] + jitter, 0, NSEC - 1).astype(jnp.int32)


def place_ends(entries, own_key, least, high):
    longest = entries.shape.index(max(entries.shape))
    spots = []
    for shift in (0, 1):
        where = [jax.random.randint(jax.random.fold_in(own_key, axis), (), 0, length) for axis, length in enumerate(entries.shape)]
        where[longest] = (where[longest] + shift) % entries.shape[longest]
        spots.append(tuple(where))
    return entries.at[spots[0]].set(least).at[spots[1]].set(high)


def level_of(rng, extent, split, least, largest):
    def one(axis_at, blocks):
        steps = jax.random.uniform(jax.random.fold_in(jax.random.fold_in(rng, 6), axis_at), (blocks,), jnp.float32, least / len(split), largest / len(split))
        return jnp.repeat(jnp.exp(steps), extent[axis_at] // blocks).reshape((-1,) + (1,) * (len(extent) - axis_at - 1))

    level = one(*split[0])
    for cut in split[1:]:
        level = level * one(*cut)
    return level


def normal_values(key, dims, width, most, pieces=(), kind=jnp.bfloat16):
    values = jax.random.normal(key, dims, jnp.float32) * width
    if len(pieces) > 0:
        values = level_of(key, dims, pieces, -0.22, 0.18) * values
    return jnp.clip(values, min=-most, max=most).astype(kind)


def setup_inputs(seed: int = 0) -> dict:
    splits = jax.random.split(jax.random.key(seed), 7)
    return {
        "volume_frac": jnp.clip(1.0 * jax.random.uniform(splits[0], (INSTANCES, NV, NY, NX), jnp.float32) ** level_of(splits[0], (INSTANCES, NV, NY, NX), ((0, 8), (1, 32)), -0.2, 0.2), 0.0, 1.0),
        "velocity_u": normal_values(splits[1], (INSTANCES, NV, NY, NX), 1.0, 6.0, ((0, 8), (1, 32)), jnp.float32),
        "velocity_v": normal_values(splits[2], (INSTANCES, NV, NY, NX), 1.0, 6.0, ((0, 8), (1, 32)), jnp.float32),
        "velocity_w": normal_values(splits[3], (INSTANCES, NV, NY, NX), 1.0, 6.0, ((0, 8), (1, 32)), jnp.float32),
        "wetted": place_ends((jax.random.randint(splits[4], (INSTANCES, NV, NY, NX), 0, 2) < 1).astype(jnp.int32), jax.random.fold_in(splits[4], 1), 0, 1),
        "section_map": draw_section_map(jax.random.fold_in(splits[6], 71), 0),
    }


SIGMA = 1.0
GRAVITY = 4.0


def coef_table(count):
    steps = jnp.arange(count, dtype=jnp.int32)
    angle = (jnp.pi / count) * steps.astype(jnp.float32)
    parity = (1 - 2 * (steps % 2)).astype(jnp.float32)
    sine = jnp.where(steps == 0, jnp.float32(1.0), jnp.sin(angle))
    spectral = jnp.where(steps == 0, jnp.float32(0.0), 0.5 * parity * jnp.cos(angle) / sine)
    return spectral + (SIGMA / count) * parity


def upwind(field, speed, axis):
    length = field.shape[axis] - 2
    lower_f = lax.slice_in_dim(field, 0, length + 1, axis=axis)
    upper_f = lax.slice_in_dim(field, 1, length + 2, axis=axis)
    face_speed = 0.5 * (lax.slice_in_dim(speed, 0, length + 1, axis=axis) + lax.slice_in_dim(speed, 1, length + 2, axis=axis))
    flux = jnp.maximum(face_speed, 0.0) * lower_f + jnp.minimum(face_speed, 0.0) * upper_f
    return lax.slice_in_dim(flux, 1, length + 1, axis=axis) - lax.slice_in_dim(flux, 0, length, axis=axis)


def pad_axis(field, axis):
    widths = [(0, 0), (0, 0), (0, 0)]
    widths[axis] = (1, 1)
    return jnp.pad(field, widths)


def reference(volume_frac, velocity_u, velocity_v, velocity_w, wetted, section_map):
    count = INSTANCES
    table = coef_table(count)
    order = jnp.arange(count, dtype=jnp.int32)
    cmatrix = table[(order[:, None] - order[None, :]) % count]
    derivative = jnp.einsum('nm,mvyx->nvyx', cmatrix, volume_frac, precision=lax.Precision.HIGHEST)
    depth = (jnp.arange(NV, dtype=jnp.int32).astype(jnp.float32) + 0.5) / jnp.float32(NV)
    lever = (jnp.arange(NY, dtype=jnp.int32).astype(jnp.float32) + 0.5) / jnp.float32(NY)
    flat_map = section_map.reshape(-1)
    factor = jnp.float32(SEC_DEV / (CV * NY * NX))

    def one_instance(items):
        alpha, speed_u, speed_v, speed_w, mask = items
        divergence = upwind(pad_axis(alpha, 0), pad_axis(speed_w, 0), 0)
        divergence = divergence + upwind(pad_axis(alpha, 1), pad_axis(speed_v, 1), 1)
        divergence = divergence + upwind(pad_axis(alpha, 2), pad_axis(speed_u, 2), 2)
        pressure = GRAVITY * depth[:, None, None] + 0.5 * (speed_u * speed_u + speed_v * speed_v + speed_w * speed_w)
        load = mask.astype(jnp.float32) * alpha * pressure
        force = jax.ops.segment_sum(load.reshape(-1), flat_map, num_segments=NSEC)
        moment = jax.ops.segment_sum((load * lever[None, :, None]).reshape(-1), flat_map, num_segments=NSEC)
        return divergence, jnp.stack([force, moment]) * factor

    divergence, loads = lax.map(one_instance, (volume_frac, velocity_u, velocity_v, velocity_w, wetted))
    return derivative + divergence, loads
```

```python
import functools
import math

import jax
import jax.numpy as jnp
from jax import lax
from jax.experimental import pallas as pl
from jax.experimental.pallas import tpu as pltpu
from jax.sharding import PartitionSpec as P

MESH = pl.DeviceIdType.MESH
F32 = jnp.float32

GRAVITY = 4.0
SIGMA = 1.0
ROOT2 = math.sqrt(2.0)

CV, NY, NX = 8, 64, 512
N_INST, N_SLAB = 8, 32
NSEC = 64
CHUNKS = 4
ROWS = NY // CHUNKS

PEERS = ((1, 0), (0, 1), (1, 1), (0, 3), (1, 3), (0, 2), (1, 2))
GROUP = ((0, 1), (1, 0), (1, 1))


def flux(speed_lo, speed_hi, lower, upper):
    f = 0.5 * (speed_lo + speed_hi)
    return jnp.maximum(f, 0.0) * lower + jnp.minimum(f, 0.0) * upper


def kernel(vf, vu, vv, vw, wet, sec, res, owned,
           a_s, u_s, v_s, w_s, m_s, s_s, got, ret, back, div, plane, halo, tile, near, far,
           in_sem, p1_send, p1_recv, p2_send, p2_recv, h_send, h_recv, l1_send, l1_recv, l2_send, l2_recv):
    inst = lax.axis_index("inst")
    slab = lax.axis_index("slab")
    xh, y = inst // 4, lax.rem(inst, 4)
    zpos, xl, core = slab // 4, lax.rem(slab // 2, 2), lax.rem(slab, 2)

    def to(dx, dy):
        return lax.rem(xh + dx, 2) * 4 + lax.rem(y + dy, 4)

    def fro(dx, dy):
        return lax.rem(xh + dx, 2) * 4 + lax.rem(y + 4 - dy, 4)

    def grp(dxl, dc):
        return zpos * 4 + lax.rem(xl + dxl, 2) * 2 + lax.rem(core + dc, 2)

    def zto(dz):
        return lax.rem(zpos + dz, N_SLAB // 4) * 4 + xl * 2 + core

    up = lax.rem(slab + 1, N_SLAB)
    down = lax.rem(slab + N_SLAB - 1, N_SLAB)
    n_z = N_SLAB // 4

    barrier = pltpu.get_barrier_semaphore()
    greeted = [(fro(dx, dy), slab) for dx, dy in PEERS]
    greeted += [(inst, up), (inst, down)]
    greeted += [(inst, grp(a, b)) for a, b in GROUP]
    greeted += [(inst, zto(n_z - dz)) for dz in range(1, n_z)]
    for who in greeted:
        pl.semaphore_signal(barrier, inc=1, device_id=who, device_id_type=MESH)

    loads = [
        pltpu.make_async_copy(src.at[0], dst, in_sem.at[i])
        for i, (src, dst) in enumerate(((vf, a_s), (vu, u_s), (vv, v_s), (vw, w_s), (wet, m_s)))
    ]
    loads.append(pltpu.make_async_copy(sec, s_s, in_sem.at[5]))
    for cp in loads:
        cp.start()
    pl.semaphore_wait(barrier, len(greeted))

    def send_out(c, _):
        rows = pl.ds(pl.multiple_of(c * ROWS, ROWS), ROWS)
        for k, (dx, dy) in enumerate(PEERS):
            peer = to(dx, dy)
            pltpu.make_async_remote_copy(
                src_ref=vf.at[0, peer, rows], dst_ref=got.at[c, k],
                send_sem=p1_send, recv_sem=p1_recv.at[c],
                device_id=(peer, slab), device_id_type=MESH,
            ).start()
        return 0

    lax.fori_loop(0, CHUNKS, send_out, 0)

    halo_cps = []
    for side, (who, layer) in enumerate(((up, CV - 1), (down, 0))):
        for q, src in enumerate((vf, vw)):
            halo_cps.append(pltpu.make_async_remote_copy(
                src_ref=src.at[0, layer], dst_ref=halo.at[side, q],
                send_sem=h_send.at[side, q], recv_sem=h_recv.at[side, q],
                device_id=(inst, who), device_id_type=MESH,
            ))
    for cp in halo_cps:
        cp.start()

    for cp in loads:
        cp.wait()

    lane = lax.broadcasted_iota(jnp.int32, (8, NX), 1)
    sub = lax.broadcasted_iota(jnp.int32, (8, NX), 0)
    base = lane // (NX // NSEC)
    total = N_SLAB * CV

    def load_rows(r, sums):
        rows = pl.ds(pl.multiple_of(r * 8, 8), 8)

        def load_layer(v, acc):
            u, vy, w = u_s[v, rows], v_s[v, rows], w_s[v, rows]
            depth = ((slab * CV + v).astype(F32) + 0.5) * (GRAVITY / total)
            pressure = depth + 0.5 * (u * u + vy * vy + w * w)
            load = m_s[v, rows].astype(F32) * a_s[v, rows] * pressure
            rel = s_s[v, rows] - base
            return tuple(a + jnp.where(rel == o, load, 0.0) for a, o in zip(acc, (-1, 0, 1)))

        acc = lax.fori_loop(0, CV, load_layer, (jnp.zeros((8, NX), F32),) * 3)
        lever = ((r * 8 + sub).astype(F32) + 0.5) * (1.0 / NY)
        return tuple(s + a for s, a in zip(sums[:3], acc)) + tuple(s + a * lever for s, a in zip(sums[3:], acc))

    sums = lax.fori_loop(0, NY // 8, load_rows, (jnp.zeros((8, NX), F32),) * 6)
    term = jnp.zeros((16, 128), F32)
    col = lax.broadcasted_iota(jnp.int32, (NX, 128), 0) // (NX // NSEC)
    secs = lax.broadcasted_iota(jnp.int32, (NX, 128), 1)
    for n, o in enumerate((-1, 0, 1)):
        pick = (col + o == secs).astype(F32)
        both = jnp.concatenate([sums[n], sums[3 + n]], axis=0)
        term = term + jnp.dot(both, pick, precision=lax.Precision.HIGHEST, preferred_element_type=F32)
    force = jnp.sum(term[:8], axis=0, keepdims=True)
    moment = jnp.sum(term[8:], axis=0, keepdims=True)
    sub128 = lax.broadcasted_iota(jnp.int32, (8, 128), 0)
    tile[0] = jnp.where(sub128 == 0, force, jnp.where(sub128 == 1, moment, 0.0)) * (2.0 / (CV * NY * NX))
    for k, (a, b) in enumerate(GROUP):
        pltpu.make_async_remote_copy(
            src_ref=tile.at[0], dst_ref=near.at[k], send_sem=l1_send, recv_sem=l1_recv,
            device_id=(inst, grp(a, b)), device_id_type=MESH,
        ).start()

    plane[...] = jnp.zeros_like(plane)
    first_lane, last_lane = lane == 0, lane == NX - 1
    first_sub, last_sub = sub == 0, sub == 7

    def one_layer(v, _):
        above = jnp.minimum(v + 1, CV - 1)
        inner = jnp.where(v < CV - 1, 1.0, 0.0)
        prev = None
        for r in range(NY // 8):
            rows = pl.ds(r * 8, 8)
            a, u, s, w = a_s[v, rows], u_s[v, rows], v_s[v, rows], w_s[v, rows]
            top = flux(w, w_s[above, rows], a, a_s[above, rows]) * inner
            d = top - plane[rows]
            plane[rows] = top
            if r < NY // 8 - 1:
                nxt = pl.ds(r * 8 + 8, 8)
                a_n, s_n = pltpu.roll(a_s[v, nxt], 7, 0), pltpu.roll(v_s[v, nxt], 7, 0)
            else:
                a_n = s_n = jnp.zeros((8, NX), F32)
            a_up = jnp.where(last_sub, a_n, pltpu.roll(a, 7, 0))
            s_up = jnp.where(last_sub, s_n, pltpu.roll(s, 7, 0))
            fy = flux(s, s_up, a, a_up)
            fy_roll = pltpu.roll(fy, 1, 0)
            if prev is None:
                low = jnp.minimum(0.5 * s, 0.0) * a
            else:
                low = prev
            d = d + (fy - jnp.where(first_sub, low, fy_roll))
            prev = fy_roll
            a_r = jnp.where(last_lane, 0.0, pltpu.roll(a, NX - 1, 1))
            u_r = jnp.where(last_lane, 0.0, pltpu.roll(u, NX - 1, 1))
            fx = flux(u, u_r, a, a_r)
            left = jnp.minimum(0.5 * u, 0.0) * a
            d = d + (fx - jnp.where(first_lane, left, pltpu.roll(fx, 1, 1)))
            div[v, rows] = d
        return 0

    lax.fori_loop(0, CV, one_layer, 0)

    pltpu.make_async_copy(near, near, l1_recv).wait()
    tile[1] = tile[0] + near[0] + near[1] + near[2]
    for dz in range(1, n_z):
        pltpu.make_async_remote_copy(
            src_ref=tile.at[1], dst_ref=far.at[dz - 1], send_sem=l2_send, recv_sem=l2_recv,
            device_id=(inst, zto(dz)), device_id_type=MESH,
        ).start()

    sig = [jnp.where(y >= k, 1.0, -1.0) for k in range(4)]
    tau = [jnp.where(y + k < 4, 0.5, -0.5) for k in range(4)]
    slot = {p: k for k, p in enumerate(PEERS)}

    def combine(c, _):
        start = pl.multiple_of(c * ROWS, ROWS)
        pltpu.make_async_copy(got.at[c], got.at[c], p1_recv.at[c]).wait()
        for r in range(ROWS // 8):
            for h in range(2):
                cols = pl.ds(h * 256, 256)
                rr = pl.ds(r * 8, 8)
                p, q = [], []
                for k in range(4):
                    if k == 0:
                        mine = a_s[inst, pl.ds(pl.multiple_of(start + r * 8, 8), 8), cols]
                    else:
                        mine = got[c, slot[(0, k)], rr, cols]
                    other = got[c, slot[(1, k)], rr, cols]
                    p.append(mine + other)
                    q.append((mine - other) * sig[k])
                even, odd = p[0] - p[2], p[3] - p[1]
                nyq = ((p[0] + p[2]) - (p[1] + p[3])) * (SIGMA / N_INST)
                half_odd, half_even = 0.5 * odd, 0.5 * even
                ps = (half_odd + nyq, -half_even - nyq, nyq - half_odd, half_even - nyq)
                qs = (
                    q[2] - ROOT2 * (q[1] + q[3]),
                    q[1] - ROOT2 * (q[0] + q[2]),
                    q[0] - ROOT2 * (q[1] - q[3]),
                    -q[3] - ROOT2 * (q[0] - q[2]),
                )
                for t in range(4):
                    qt = qs[t] * tau[t]
                    if t == 0:
                        back[c, 7, rr, cols] = ps[t] + qt
                    else:
                        ret[c, slot[(0, t)], rr, cols] = ps[t] + qt
                    ret[c, slot[(1, t)], rr, cols] = ps[t] - qt
        for k, (dx, dy) in enumerate(PEERS):
            pltpu.make_async_remote_copy(
                src_ref=ret.at[c, k], dst_ref=back.at[c, k],
                send_sem=p2_send, recv_sem=p2_recv.at[c],
                device_id=(to(dx, dy), slab), device_id_type=MESH,
            ).start()
        return 0

    lax.fori_loop(0, CHUNKS, combine, 0)

    for cp in halo_cps:
        cp.wait()
    keep_lo = jnp.where(slab > 0, 1.0, 0.0)
    keep_hi = jnp.where(slab < N_SLAB - 1, 1.0, 0.0)

    def edges(r, _):
        rows = pl.ds(pl.multiple_of(r * 8, 8), 8)
        lo = flux(halo[0, 1, rows] * keep_lo, w_s[0, rows], halo[0, 0, rows] * keep_lo, a_s[0, rows])
        hi = flux(w_s[CV - 1, rows], halo[1, 1, rows] * keep_hi, a_s[CV - 1, rows], halo[1, 0, rows] * keep_hi)
        div[0, rows] = div[0, rows] - lo
        div[CV - 1, rows] = div[CV - 1, rows] + hi
        return 0

    lax.fori_loop(0, NY // 8, edges, 0)

    pltpu.make_async_copy(far, far, l2_recv).wait()
    whole = tile[1]
    for dz in range(1, n_z):
        whole = whole + far[dz - 1]
    lane128 = lax.broadcasted_iota(jnp.int32, (8, 128), 1)
    for e in range(2):
        one = jnp.sum(jnp.where(lane128 == slab * 2 + e, whole, 0.0), axis=1, keepdims=True)
        owned[0, :, e:e + 1] = one[:2]

    layer_of = [fro(dx, dy) for dx, dy in PEERS] + [inst]

    def finish(c, _):
        start = pl.multiple_of(c * ROWS, ROWS)
        rows = pl.ds(start, ROWS)
        pltpu.make_async_copy(back.at[c, pl.ds(0, 7)], back.at[c, pl.ds(0, 7)], p2_recv.at[c]).wait()
        for k, layer in enumerate(layer_of):
            res[0, layer, rows] = div[layer, rows] + back[c, k]
        return 0

    lax.fori_loop(0, CHUNKS, finish, 0)

    pltpu.make_async_copy(a_s.at[pl.ds(0, 7)], a_s.at[pl.ds(0, 7)], p1_send).wait()
    pltpu.make_async_copy(ret, ret, p2_send).wait()
    pltpu.make_async_copy(near, near, l1_send).wait()
    pltpu.make_async_copy(far, far, l2_send).wait()


def on_device(*args):
    hbm, vmem = pl.BlockSpec(memory_space=pltpu.HBM), pl.BlockSpec(memory_space=pltpu.VMEM)
    block = (CV, NY, NX)
    dma = pltpu.SemaphoreType.DMA
    return pl.pallas_call(
        kernel,
        out_shape=(jax.ShapeDtypeStruct((1,) + block, F32), jax.ShapeDtypeStruct((1, 2, 2), F32)),
        in_specs=[hbm] * 6,
        out_specs=(vmem, vmem),
        scratch_shapes=[
            pltpu.VMEM(block, F32), pltpu.VMEM(block, F32), pltpu.VMEM(block, F32), pltpu.VMEM(block, F32),
            pltpu.VMEM(block, jnp.int32), pltpu.VMEM(block, jnp.int32),
            pltpu.VMEM((CHUNKS, 7, ROWS, NX), F32),
            pltpu.VMEM((CHUNKS, 7, ROWS, NX), F32),
            pltpu.VMEM((CHUNKS, 8, ROWS, NX), F32),
            pltpu.VMEM(block, F32),
            pltpu.VMEM((NY, NX), F32),
            pltpu.VMEM((2, 2, NY, NX), F32),
            pltpu.VMEM((2, 8, 128), F32), pltpu.VMEM((3, 8, 128), F32), pltpu.VMEM((N_SLAB // 4 - 1, 8, 128), F32),
            dma((6,)), dma, dma((CHUNKS,)), dma, dma((CHUNKS,)), dma((2, 2)), dma((2, 2)),
            dma, dma, dma, dma,
        ],
        compiler_params=pltpu.CompilerParams(
            collective_id=0, has_side_effects=True, vmem_limit_bytes=62 << 20
        ),
        cost_estimate=pl.CostEstimate(flops=20_000_000, bytes_accessed=8 << 20, transcendentals=0),
    )(*args)


def solution(mesh):
    placed = (
        P("inst", "slab", None, None),
        P("inst", "slab", None, None),
        P("inst", "slab", None, None),
        P("inst", "slab", None, None),
        P("inst", "slab", None, None),
        P("slab", None, None),
    )
    return jax.shard_map(
        on_device,
        mesh=mesh,
        in_specs=placed,
        out_specs=(P("inst", "slab", None, None), P("inst", None, "slab")),
        check_vma=False,
    )
```

```python
import functools
import math

import jax
import jax.numpy as jnp
from jax import lax
from jax.experimental import pallas as pl
from jax.experimental.pallas import tpu as pltpu
from jax.sharding import PartitionSpec as P

MESH = pl.DeviceIdType.MESH
F32 = jnp.float32

GRAVITY = 4.0
SIGMA = 1.0
ROOT2 = math.sqrt(2.0)

CV, NY, NX = 8, 64, 512
N_INST, N_SLAB = 8, 32
NSEC = 64
CHUNKS = 4
ROWS = NY // CHUNKS

PEERS = ((1, 0), (0, 1), (1, 1), (0, 3), (1, 3), (0, 2), (1, 2))
GROUP = ((0, 1), (1, 0), (1, 1))


def flux(speed_lo, speed_hi, lower, upper):
    f = 0.5 * (speed_lo + speed_hi)
    return jnp.maximum(f, 0.0) * lower + jnp.minimum(f, 0.0) * upper


def kernel(vf, vu, vv, vw, wet, sec, res, owned,
           a_s, u_s, v_s, w_s, m_s, s_s, got, ret, back, div, plane, halo, tile, near, far,
           in_sem, p1_send, p1_recv, p2_send, p2_recv, h_send, h_recv, l1_send, l1_recv, l2_send, l2_recv, word):
    inst = lax.axis_index("inst")
    slab = lax.axis_index("slab")
    xh, y = inst // 4, lax.rem(inst, 4)
    zpos, xl, core = slab // 4, lax.rem(slab // 2, 2), lax.rem(slab, 2)

    def to(dx, dy):
        return lax.rem(xh + dx, 2) * 4 + lax.rem(y + dy, 4)

    def fro(dx, dy):
        return lax.rem(xh + dx, 2) * 4 + lax.rem(y + 4 - dy, 4)

    def zto(dz):
        return lax.rem(zpos + dz, n_z) * 4 + xl * 2 + core

    def grp(dxl, dc):
        return zpos * 4 + lax.rem(xl + dxl, 2) * 2 + lax.rem(core + dc, 2)

    n_z = N_SLAB // 4
    line = ((slab < N_SLAB - 1, slab + 1), (slab > 0, slab - 1))
    zline = ((zpos < n_z - 1, slab + 4), (zpos > 0, slab - 4))

    barrier = pltpu.get_barrier_semaphore()
    greeted = [(fro(dx, dy), slab) for dx, dy in PEERS]
    greeted += [(inst, grp(a, b)) for a, b in GROUP]
    expected = len(greeted)
    for who in greeted:
        pl.semaphore_signal(barrier, inc=1, device_id=who, device_id_type=MESH)
    for there, who in line + zline:
        expected = expected + there.astype(jnp.int32)

        @pl.when(there)
        def _():
            pl.semaphore_signal(barrier, inc=1, device_id=(inst, who), device_id_type=MESH)

    loads = [
        pltpu.make_async_copy(src.at[0], dst, in_sem.at[i])
        for i, (src, dst) in enumerate(((vf, a_s), (vu, u_s), (vv, v_s), (vw, w_s), (wet, m_s)))
    ]
    loads.append(pltpu.make_async_copy(sec, s_s, in_sem.at[5]))
    for cp in loads:
        cp.start()
    pl.semaphore_wait(barrier, expected)

    def send_out(c, _):
        rows = pl.ds(pl.multiple_of(c * ROWS, ROWS), ROWS)
        for k, (dx, dy) in enumerate(PEERS):
            peer = to(dx, dy)
            pltpu.make_async_remote_copy(
                src_ref=vf.at[0, peer, rows], dst_ref=got.at[c, k],
                send_sem=p1_send, recv_sem=p1_recv.at[c],
                device_id=(peer, slab), device_id_type=MESH,
            ).start()
        return 0

    lax.fori_loop(0, CHUNKS // 2, send_out, 0)

    def pass_word(way):
        @pl.when(zline[1 - way][0])
        def _():
            pl.semaphore_wait(word.at[way], 1)

        @pl.when(zline[way][0])
        def _():
            pl.semaphore_signal(word.at[way], inc=1, device_id=(inst, zline[way][1]), device_id_type=MESH)

    def spread():
        for dz in range(1, n_z):
            pltpu.make_async_remote_copy(
                src_ref=tile.at[1], dst_ref=far.at[dz - 1], send_sem=l2_send, recv_sem=l2_recv,
                device_id=(inst, zto(dz)), device_id_type=MESH,
            ).start()

    pass_word(0)

    @pl.when(zpos >= n_z // 2)
    def _():
        pass_word(1)

    for cp in loads:
        cp.wait()

    lane = lax.broadcasted_iota(jnp.int32, (8, NX), 1)
    sub = lax.broadcasted_iota(jnp.int32, (8, NX), 0)
    base = lane // (NX // NSEC)
    total = N_SLAB * CV

    def load_rows(r, sums):
        rows = pl.ds(pl.multiple_of(r * 8, 8), 8)

        def load_layer(v, acc):
            u, vy, w = u_s[v, rows], v_s[v, rows], w_s[v, rows]
            depth = ((slab * CV + v).astype(F32) + 0.5) * (GRAVITY / total)
            pressure = depth + 0.5 * (u * u + vy * vy + w * w)
            load = m_s[v, rows].astype(F32) * a_s[v, rows] * pressure
            rel = s_s[v, rows] - base
            return tuple(a + jnp.where(rel == o, load, 0.0) for a, o in zip(acc, (-1, 0, 1)))

        acc = lax.fori_loop(0, CV, load_layer, (jnp.zeros((8, NX), F32),) * 3)
        lever = ((r * 8 + sub).astype(F32) + 0.5) * (1.0 / NY)
        return tuple(s + a for s, a in zip(sums[:3], acc)) + tuple(s + a * lever for s, a in zip(sums[3:], acc))

    sums = lax.fori_loop(0, NY // 8, load_rows, (jnp.zeros((8, NX), F32),) * 6)
    term = jnp.zeros((16, 128), F32)
    col = lax.broadcasted_iota(jnp.int32, (NX, 128), 0) // (NX // NSEC)
    secs = lax.broadcasted_iota(jnp.int32, (NX, 128), 1)
    for n, o in enumerate((-1, 0, 1)):
        pick = (col + o == secs).astype(F32)
        both = jnp.concatenate([sums[n], sums[3 + n]], axis=0)
        term = term + jnp.dot(both, pick, precision=lax.Precision.HIGHEST, preferred_element_type=F32)
    force = jnp.sum(term[:8], axis=0, keepdims=True)
    moment = jnp.sum(term[8:], axis=0, keepdims=True)
    sub128 = lax.broadcasted_iota(jnp.int32, (8, 128), 0)
    tile[0] = jnp.where(sub128 == 0, force, jnp.where(sub128 == 1, moment, 0.0)) * (2.0 / (CV * NY * NX))
    for k, (a, b) in enumerate(GROUP):
        pltpu.make_async_remote_copy(
            src_ref=tile.at[0], dst_ref=near.at[k], send_sem=l1_send, recv_sem=l1_recv,
            device_id=(inst, grp(a, b)), device_id_type=MESH,
        ).start()

    lax.fori_loop(CHUNKS // 2, CHUNKS, send_out, 0)

    def halo_copies(side):
        layer = 0 if side else CV - 1
        return [
            pltpu.make_async_remote_copy(
                src_ref=src.at[0, layer], dst_ref=halo.at[side, q],
                send_sem=h_send.at[side, q], recv_sem=h_recv.at[side, q],
                device_id=(inst, line[side][1]), device_id_type=MESH,
            )
            for q, src in enumerate((vf, vw))
        ]

    for side in range(2):
        @pl.when(line[side][0])
        def _():
            for cp in halo_copies(side):
                cp.start()

        @pl.when(jnp.logical_not(line[1 - side][0]))
        def _():
            halo[side] = jnp.zeros((2, NY, NX), F32)

    plane[...] = jnp.zeros_like(plane)
    first_lane, last_lane = lane == 0, lane == NX - 1
    first_sub, last_sub = sub == 0, sub == 7

    def one_layer(v, _):
        above = jnp.minimum(v + 1, CV - 1)
        inner = jnp.where(v < CV - 1, 1.0, 0.0)
        prev = None
        for r in range(NY // 8):
            rows = pl.ds(r * 8, 8)
            a, u, s, w = a_s[v, rows], u_s[v, rows], v_s[v, rows], w_s[v, rows]
            top = flux(w, w_s[above, rows], a, a_s[above, rows]) * inner
            d = top - plane[rows]
            plane[rows] = top
            if r < NY // 8 - 1:
                nxt = pl.ds(r * 8 + 8, 8)
                a_n, s_n = pltpu.roll(a_s[v, nxt], 7, 0), pltpu.roll(v_s[v, nxt], 7, 0)
            else:
                a_n = s_n = jnp.zeros((8, NX), F32)
            a_up = jnp.where(last_sub, a_n, pltpu.roll(a, 7, 0))
            s_up = jnp.where(last_sub, s_n, pltpu.roll(s, 7, 0))
            fy = flux(s, s_up, a, a_up)
            fy_roll = pltpu.roll(fy, 1, 0)
            if prev is None:
                low = jnp.minimum(0.5 * s, 0.0) * a
            else:
                low = prev
            d = d + (fy - jnp.where(first_sub, low, fy_roll))
            prev = fy_roll
            a_r = jnp.where(last_lane, 0.0, pltpu.roll(a, NX - 1, 1))
            u_r = jnp.where(last_lane, 0.0, pltpu.roll(u, NX - 1, 1))
            fx = flux(u, u_r, a, a_r)
            left = jnp.minimum(0.5 * u, 0.0) * a
            d = d + (fx - jnp.where(first_lane, left, pltpu.roll(fx, 1, 1)))
            div[v, rows] = d
        return 0

    lax.fori_loop(0, CV, one_layer, 0)

    pltpu.make_async_copy(near, near, l1_recv).wait()
    tile[1] = tile[0] + near[0] + near[1] + near[2]

    @pl.when(zpos >= n_z // 2)
    def _():
        spread()

    sig = [jnp.where(y >= k, 1.0, -1.0) for k in range(4)]
    tau = [jnp.where(y + k < 4, 0.5, -0.5) for k in range(4)]
    slot = {p: k for k, p in enumerate(PEERS)}

    def combine(c, _):
        start = pl.multiple_of(c * ROWS, ROWS)
        pltpu.make_async_copy(got.at[c], got.at[c], p1_recv.at[c]).wait()
        for r in range(ROWS // 8):
            for h in range(2):
                cols = pl.ds(h * 256, 256)
                rr = pl.ds(r * 8, 8)
                p, q = [], []
                for k in range(4):
                    if k == 0:
                        mine = a_s[inst, pl.ds(pl.multiple_of(start + r * 8, 8), 8), cols]
                    else:
                        mine = got[c, slot[(0, k)], rr, cols]
                    other = got[c, slot[(1, k)], rr, cols]
                    p.append(mine + other)
                    q.append((mine - other) * sig[k])
                even, odd = p[0] - p[2], p[3] - p[1]
                nyq = ((p[0] + p[2]) - (p[1] + p[3])) * (SIGMA / N_INST)
                half_odd, half_even = 0.5 * odd, 0.5 * even
                ps = (half_odd + nyq, -half_even - nyq, nyq - half_odd, half_even - nyq)
                qs = (
                    q[2] - ROOT2 * (q[1] + q[3]),
                    q[1] - ROOT2 * (q[0] + q[2]),
                    q[0] - ROOT2 * (q[1] - q[3]),
                    -q[3] - ROOT2 * (q[0] - q[2]),
                )
                for t in range(4):
                    qt = qs[t] * tau[t]
                    if t == 0:
                        back[c, 7, rr, cols] = ps[t] + qt
                    else:
                        ret[c, slot[(0, t)], rr, cols] = ps[t] + qt
                    ret[c, slot[(1, t)], rr, cols] = ps[t] - qt
        for k, (dx, dy) in enumerate(PEERS):
            pltpu.make_async_remote_copy(
                src_ref=ret.at[c, k], dst_ref=back.at[c, k],
                send_sem=p2_send, recv_sem=p2_recv.at[c],
                device_id=(to(dx, dy), slab), device_id_type=MESH,
            ).start()
        return 0

    lax.fori_loop(0, CHUNKS, combine, 0)

    @pl.when(zpos < n_z // 2)
    def _():
        pass_word(1)
        spread()


    for side in range(2):
        @pl.when(line[side][0])
        def _():
            for cp in halo_copies(side):
                cp.wait_send()

        @pl.when(line[1 - side][0])
        def _():
            for cp in halo_copies(side):
                cp.wait_recv()

    def edges(r, _):
        rows = pl.ds(pl.multiple_of(r * 8, 8), 8)
        lo = flux(halo[0, 1, rows], w_s[0, rows], halo[0, 0, rows], a_s[0, rows])
        hi = flux(w_s[CV - 1, rows], halo[1, 1, rows], a_s[CV - 1, rows], halo[1, 0, rows])
        div[0, rows] = div[0, rows] - lo
        div[CV - 1, rows] = div[CV - 1, rows] + hi
        return 0

    lax.fori_loop(0, NY // 8, edges, 0)

    layer_of = [fro(dx, dy) for dx, dy in PEERS] + [inst]

    def finish(c, _):
        start = pl.multiple_of(c * ROWS, ROWS)
        rows = pl.ds(start, ROWS)
        pltpu.make_async_copy(back.at[c, pl.ds(0, 7)], back.at[c, pl.ds(0, 7)], p2_recv.at[c]).wait()
        for k, layer in enumerate(layer_of):
            res[0, layer, rows] = div[layer, rows] + back[c, k]
        return 0

    lax.fori_loop(0, CHUNKS, finish, 0)

    pltpu.make_async_copy(far, far, l2_recv).wait()
    whole = tile[1]
    for dz in range(1, n_z):
        whole = whole + far[dz - 1]
    lane128 = lax.broadcasted_iota(jnp.int32, (8, 128), 1)
    for e in range(2):
        one = jnp.sum(jnp.where(lane128 == slab * 2 + e, whole, 0.0), axis=1, keepdims=True)
        owned[0, :, e:e + 1] = one[:2]


    pltpu.make_async_copy(a_s.at[pl.ds(0, 7)], a_s.at[pl.ds(0, 7)], p1_send).wait()
    pltpu.make_async_copy(ret, ret, p2_send).wait()
    pltpu.make_async_copy(near, near, l1_send).wait()
    pltpu.make_async_copy(far, far, l2_send).wait()


def on_device(*args):
    hbm, vmem = pl.BlockSpec(memory_space=pltpu.HBM), pl.BlockSpec(memory_space=pltpu.VMEM)
    block = (CV, NY, NX)
    dma = pltpu.SemaphoreType.DMA
    return pl.pallas_call(
        kernel,
        out_shape=(jax.ShapeDtypeStruct((1,) + block, F32), jax.ShapeDtypeStruct((1, 2, 2), F32)),
        in_specs=[hbm] * 6,
        out_specs=(vmem, vmem),
        scratch_shapes=[
            pltpu.VMEM(block, F32), pltpu.VMEM(block, F32), pltpu.VMEM(block, F32), pltpu.VMEM(block, F32),
            pltpu.VMEM(block, jnp.int32), pltpu.VMEM(block, jnp.int32),
            pltpu.VMEM((CHUNKS, 7, ROWS, NX), F32),
            pltpu.VMEM((CHUNKS, 7, ROWS, NX), F32),
            pltpu.VMEM((CHUNKS, 8, ROWS, NX), F32),
            pltpu.VMEM(block, F32),
            pltpu.VMEM((NY, NX), F32),
            pltpu.VMEM((2, 2, NY, NX), F32),
            pltpu.VMEM((2, 8, 128), F32), pltpu.VMEM((3, 8, 128), F32), pltpu.VMEM((N_SLAB // 4 - 1, 8, 128), F32),
            dma((6,)), dma, dma((CHUNKS,)), dma, dma((CHUNKS,)), dma((2, 2)), dma((2, 2)),
            dma, dma, dma, dma, pltpu.SemaphoreType.REGULAR((2,)),
        ],
        compiler_params=pltpu.CompilerParams(
            collective_id=0, has_side_effects=True, vmem_limit_bytes=52 << 20
        ),
        cost_estimate=pl.CostEstimate(flops=20_000_000, bytes_accessed=8 << 20, transcendentals=0),
    )(*args)


def solution(mesh):
    placed = (
        P("inst", "slab", None, None),
        P("inst", "slab", None, None),
        P("inst", "slab", None, None),
        P("inst", "slab", None, None),
        P("inst", "slab", None, None),
        P("slab", None, None),
    )
    return jax.shard_map(
        on_device,
        mesh=mesh,
        in_specs=placed,
        out_specs=(P("inst", "slab", None, None), P("inst", None, "slab")),
        check_vma=False,
    )
```

```python
import functools
import math

import jax
import jax.numpy as jnp
from jax import lax
from jax.experimental import pallas as pl
from jax.experimental.pallas import tpu as pltpu
from jax.sharding import PartitionSpec as P

MESH = pl.DeviceIdType.MESH
F32 = jnp.float32

GRAVITY = 4.0
SIGMA = 1.0
ROOT2 = math.sqrt(2.0)

CV, NY, NX = 8, 64, 512
N_INST, N_SLAB = 8, 32
NSEC = 64
STRIP = NY // N_INST
PARTS = ((1, 3), (4, 3))
TOP = CV - 1

PEERS = ((1, 0), (0, 1), (1, 1), (0, 3), (1, 3), (0, 2), (1, 2))
GROUP = ((0, 1), (1, 0), (1, 1))


def flux(speed_lo, speed_hi, lower, upper):
    f = 0.5 * (speed_lo + speed_hi)
    return jnp.maximum(f, 0.0) * lower + jnp.minimum(f, 0.0) * upper


def kernel(vf, vu, vv, vw, wet, sec, res, owned,
           a_s, u_s, v_s, w_s, m_s, s_s, got, ret, back, w_got, j_got, j_ret, div, plane, halo, tile, near, far,
           in_sem, p1_send, p1_recv, p2_send, p2_recv, first_send, w_send, w_recv, j_send, j_recv, r_send,
           h_send, h_recv, l1_send, l1_recv, l2_send, l2_recv, word):
    inst = lax.axis_index("inst")
    slab = lax.axis_index("slab")
    xh, y = inst // 4, lax.rem(inst, 4)
    zpos, xl, core = slab // 4, lax.rem(slab // 2, 2), lax.rem(slab, 2)

    def to(dx, dy):
        return lax.rem(xh + dx, 2) * 4 + lax.rem(y + dy, 4)

    def fro(dx, dy):
        return lax.rem(xh + dx, 2) * 4 + lax.rem(y + 4 - dy, 4)

    def zto(dz):
        return lax.rem(zpos + dz, n_z) * 4 + xl * 2 + core

    def grp(dxl, dc):
        return zpos * 4 + lax.rem(xl + dxl, 2) * 2 + lax.rem(core + dc, 2)

    n_z = N_SLAB // 4
    zline = ((zpos < n_z - 1, slab + 4), (zpos > 0, slab - 4))
    across = slab + 2 * core - 1
    paired = jnp.logical_and(across >= 0, across < N_SLAB)
    joint = jnp.logical_and(core == 1, paired)
    lent = jnp.logical_and(core == 0, paired)
    own_first = jnp.logical_not(lent)

    barrier = pltpu.get_barrier_semaphore()
    greeted = [(fro(dx, dy), slab) for dx, dy in PEERS]
    greeted += [(inst, grp(a, b)) for a, b in GROUP]
    expected = len(greeted)
    for who in greeted:
        pl.semaphore_signal(barrier, inc=1, device_id=who, device_id_type=MESH)
    for there, who in zline:
        expected = expected + there.astype(jnp.int32)

        @pl.when(there)
        def _():
            pl.semaphore_signal(barrier, inc=1, device_id=(inst, who), device_id_type=MESH)

    expected = expected + N_INST * paired.astype(jnp.int32)

    @pl.when(paired)
    def _():
        for n in range(N_INST):
            pl.semaphore_signal(barrier, inc=1, device_id=(n, across), device_id_type=MESH)

    loads = [
        pltpu.make_async_copy(src.at[0], dst, in_sem.at[i])
        for i, (src, dst) in enumerate(((vf, a_s), (vu, u_s), (vv, v_s), (vw, w_s), (wet, m_s)))
    ]
    loads.append(pltpu.make_async_copy(sec, s_s, in_sem.at[5]))
    for cp in loads:
        cp.start()
    pl.semaphore_wait(barrier, expected)

    def remote(src, dst, send, recv, where):
        return pltpu.make_async_remote_copy(
            src_ref=src, dst_ref=dst, send_sem=send, recv_sem=recv, device_id=where, device_id_type=MESH
        )

    def strip(n):
        return pl.ds(pl.multiple_of(n * STRIP, STRIP), STRIP)

    def send_out(part, first, count):
        layers = pl.ds(first, count)
        for k, (dx, dy) in enumerate(PEERS):
            peer = to(dx, dy)
            remote(vf.at[0, layers, strip(peer)], got.at[layers, k], p1_send, p1_recv.at[part], (peer, slab)).start()

    n_parts = len(PARTS)
    part_top, part_first = n_parts, n_parts + 1
    everyone = PEERS + ((0, 0),)

    @pl.when(lent)
    def _():
        for k, (dx, dy) in enumerate(everyone):
            peer = to(dx, dy)
            for q, src in enumerate((vf, vw)):
                remote(src.at[0, 0, strip(peer)], j_got.at[q, k], j_send, j_recv, (peer, across)).start()

    send_out(0, *PARTS[0])
    send_out(part_top, TOP, 1)

    @pl.when(joint)
    def _():
        for k, (dx, dy) in enumerate(PEERS):
            peer = to(dx, dy)
            remote(vw.at[0, TOP, strip(peer)], w_got.at[k], w_send, w_recv, (peer, slab)).start()

    @pl.when(jnp.logical_not(joint))
    def _():
        w_got[...] = jnp.zeros_like(w_got)
        j_got[...] = jnp.zeros_like(j_got)

    def pass_word(way):
        @pl.when(zline[1 - way][0])
        def _():
            pl.semaphore_wait(word.at[way], 1)

        @pl.when(zline[way][0])
        def _():
            pl.semaphore_signal(word.at[way], inc=1, device_id=(inst, zline[way][1]), device_id_type=MESH)

    def spread():
        for dz in range(1, n_z):
            pltpu.make_async_remote_copy(
                src_ref=tile.at[1], dst_ref=far.at[dz - 1], send_sem=l2_send, recv_sem=l2_recv,
                device_id=(inst, zto(dz)), device_id_type=MESH,
            ).start()

    pass_word(0)

    @pl.when(zpos >= n_z // 2)
    def _():
        pass_word(1)

    for cp in loads:
        cp.wait()

    lane = lax.broadcasted_iota(jnp.int32, (8, NX), 1)
    sub = lax.broadcasted_iota(jnp.int32, (8, NX), 0)
    base = lane // (NX // NSEC)
    total = N_SLAB * CV

    def load_rows(r, sums):
        rows = pl.ds(pl.multiple_of(r * 8, 8), 8)

        def load_layer(v, acc):
            u, vy, w = u_s[v, rows], v_s[v, rows], w_s[v, rows]
            depth = ((slab * CV + v).astype(F32) + 0.5) * (GRAVITY / total)
            pressure = depth + 0.5 * (u * u + vy * vy + w * w)
            load = m_s[v, rows].astype(F32) * a_s[v, rows] * pressure
            rel = s_s[v, rows] - base
            return tuple(a + jnp.where(rel == o, load, 0.0) for a, o in zip(acc, (-1, 0, 1)))

        acc = lax.fori_loop(0, CV, load_layer, (jnp.zeros((8, NX), F32),) * 3)
        lever = ((r * 8 + sub).astype(F32) + 0.5) * (1.0 / NY)
        return tuple(s + a for s, a in zip(sums[:3], acc)) + tuple(s + a * lever for s, a in zip(sums[3:], acc))

    sums = lax.fori_loop(0, NY // 8, load_rows, (jnp.zeros((8, NX), F32),) * 6)
    term = jnp.zeros((16, 128), F32)
    col = lax.broadcasted_iota(jnp.int32, (NX, 128), 0) // (NX // NSEC)
    secs = lax.broadcasted_iota(jnp.int32, (NX, 128), 1)
    for n, o in enumerate((-1, 0, 1)):
        pick = (col + o == secs).astype(F32)
        both = jnp.concatenate([sums[n], sums[3 + n]], axis=0)
        term = term + jnp.dot(both, pick, precision=lax.Precision.HIGHEST, preferred_element_type=F32)
    force = jnp.sum(term[:8], axis=0, keepdims=True)
    moment = jnp.sum(term[8:], axis=0, keepdims=True)
    sub128 = lax.broadcasted_iota(jnp.int32, (8, 128), 0)
    tile[0] = jnp.where(sub128 == 0, force, jnp.where(sub128 == 1, moment, 0.0)) * (2.0 / (CV * NY * NX))
    for k, (a, b) in enumerate(GROUP):
        pltpu.make_async_remote_copy(
            src_ref=tile.at[0], dst_ref=near.at[k], send_sem=l1_send, recv_sem=l1_recv,
            device_id=(inst, grp(a, b)), device_id_type=MESH,
        ).start()

    @pl.when(own_first)
    def _():
        for k, (dx, dy) in enumerate(PEERS):
            peer = to(dx, dy)
            remote(vf.at[0, 0, strip(peer)], got.at[0, k], first_send, p1_recv.at[part_first], (peer, slab)).start()

    for part in range(1, n_parts):
        send_out(part, *PARTS[part])

    inner_layer = TOP - TOP * core
    halo_cps = [
        remote(src.at[0, inner_layer], halo.at[core, q], h_send.at[q], h_recv.at[q], (inst, slab + 1 - 2 * core))
        for q, src in enumerate((vf, vw))
    ]
    for cp in halo_cps:
        cp.start()
    halo[core] = jnp.zeros((2, NY, NX), F32)

    plane[...] = jnp.zeros_like(plane)
    first_lane, last_lane = lane == 0, lane == NX - 1
    first_sub, last_sub = sub == 0, sub == 7

    def one_layer(v, _):
        above = jnp.minimum(v + 1, CV - 1)
        inner = jnp.where(v < CV - 1, 1.0, 0.0)
        prev = None
        for r in range(NY // 8):
            rows = pl.ds(r * 8, 8)
            a, u, s, w = a_s[v, rows], u_s[v, rows], v_s[v, rows], w_s[v, rows]
            top = flux(w, w_s[above, rows], a, a_s[above, rows]) * inner
            d = top - plane[rows]
            plane[rows] = top
            if r < NY // 8 - 1:
                nxt = pl.ds(r * 8 + 8, 8)
                a_n, s_n = pltpu.roll(a_s[v, nxt], 7, 0), pltpu.roll(v_s[v, nxt], 7, 0)
            else:
                a_n = s_n = jnp.zeros((8, NX), F32)
            a_up = jnp.where(last_sub, a_n, pltpu.roll(a, 7, 0))
            s_up = jnp.where(last_sub, s_n, pltpu.roll(s, 7, 0))
            fy = flux(s, s_up, a, a_up)
            fy_roll = pltpu.roll(fy, 1, 0)
            if prev is None:
                low = jnp.minimum(0.5 * s, 0.0) * a
            else:
                low = prev
            d = d + (fy - jnp.where(first_sub, low, fy_roll))
            prev = fy_roll
            a_r = jnp.where(last_lane, 0.0, pltpu.roll(a, NX - 1, 1))
            u_r = jnp.where(last_lane, 0.0, pltpu.roll(u, NX - 1, 1))
            fx = flux(u, u_r, a, a_r)
            left = jnp.minimum(0.5 * u, 0.0) * a
            d = d + (fx - jnp.where(first_lane, left, pltpu.roll(fx, 1, 1)))
            div[v, rows] = d
        return 0

    lax.fori_loop(0, CV, one_layer, 0)

    pltpu.make_async_copy(near, near, l1_recv).wait()
    tile[1] = tile[0] + near[0] + near[1] + near[2]

    @pl.when(zpos >= n_z // 2)
    def _():
        spread()

    sig = [jnp.where(y >= k, 1.0, -1.0) for k in range(4)]
    tau = [jnp.where(y + k < 4, 0.5, -0.5) for k in range(4)]
    slot = {p: k for k, p in enumerate(everyone)}
    mine = strip(inst)

    def circulant(value):
        p = [value(0, k) + value(1, k) for k in range(4)]
        q = [(value(0, k) - value(1, k)) * sig[k] for k in range(4)]
        half_odd, half_even = 0.5 * (p[3] - p[1]), 0.5 * (p[0] - p[2])
        nyq = ((p[0] + p[2]) - (p[1] + p[3])) * (SIGMA / N_INST)
        ps = (half_odd + nyq, -half_even - nyq, nyq - half_odd, half_even - nyq)
        qs = (
            q[2] - ROOT2 * (q[1] + q[3]),
            q[1] - ROOT2 * (q[0] + q[2]),
            q[0] - ROOT2 * (q[1] - q[3]),
            -q[3] - ROOT2 * (q[0] - q[2]),
        )
        out = {}
        for t in range(4):
            qt = qs[t] * tau[t]
            out[(0, t)] = ps[t] + qt
            out[(1, t)] = ps[t] - qt
        return out

    halves = [pl.ds(h * 256, 256) for h in range(2)]

    def arrived(layer, cols):
        def value(e, k):
            if (e, k) == (0, 0):
                return a_s[layer, mine, cols]
            return got[layer, slot[(e, k)], :, cols]

        return value

    def put(layer, cols, out):
        for p, value in out.items():
            if p == (0, 0):
                back[layer, 7, :, cols] = value
            else:
                ret[layer, slot[p], :, cols] = value

    def all_of(ref, sem):
        pltpu.make_async_copy(ref, ref, sem).wait()

    def one_strip(layer, _):
        for cols in halves:
            put(layer, cols, circulant(arrived(layer, cols)))
        return 0

    def send_back(part, first, count, send):
        layers = pl.ds(first, count)
        for k, (dx, dy) in enumerate(PEERS):
            remote(ret.at[layers, k], back.at[layers, k], send, p2_recv.at[part], (to(dx, dy), slab)).start()

    def combine(part, first, count):
        all_of(got.at[pl.ds(first, count)], p1_recv.at[part])
        lax.fori_loop(first, first + count, one_strip, 0)
        send_back(part, first, count, p2_send)

    def combine_top():
        all_of(got.at[TOP], p1_recv.at[part_top])

        @pl.when(joint)
        def _():
            all_of(w_got, w_recv)
            all_of(j_got, j_recv)

        use = jnp.where(joint, 1.0, 0.0)
        for cols in halves:
            alpha = arrived(TOP, cols)
            face = {}
            for e, k in everyone:
                w = w_s[TOP, mine, cols] if (e, k) == (0, 0) else w_got[slot[(e, k)], :, cols]
                n = slot[(e, k)]
                face[(e, (4 - k) % 4)] = use * flux(w, j_got[1, n, :, cols], alpha(e, k), j_got[0, n, :, cols])
            out = circulant(alpha)
            put(TOP, cols, {p: out[p] + face[p] for p in out})
            out = circulant(lambda e, k: j_got[0, slot[(e, k)], :, cols])
            for p in out:
                j_ret[slot[p], :, cols] = out[p] - face[p]
        send_back(part_top, TOP, 1, p2_send)

        @pl.when(joint)
        def _():
            for k, (dx, dy) in enumerate(everyone):
                remote(j_ret.at[k], back.at[0, k], r_send, p2_recv.at[part_first], (to(dx, dy), across)).start()

    combine(0, *PARTS[0])

    @pl.when(own_first)
    def _():
        all_of(got.at[0], p1_recv.at[part_first])
        one_strip(0, 0)
        send_back(part_first, 0, 1, first_send)

    for part in range(1, n_parts):
        combine(part, *PARTS[part])
    combine_top()

    @pl.when(zpos < n_z // 2)
    def _():
        pass_word(1)
        spread()


    for cp in halo_cps:
        cp.wait()
    use_lo = jnp.where(jnp.logical_or(core == 1, slab == 0), 1.0, 0.0)
    use_hi = jnp.where(jnp.logical_or(core == 0, slab == N_SLAB - 1), 1.0, 0.0)

    def edges(r, _):
        rows = pl.ds(pl.multiple_of(r * 8, 8), 8)
        lo = flux(halo[0, 1, rows], w_s[0, rows], halo[0, 0, rows], a_s[0, rows])
        hi = flux(w_s[TOP, rows], halo[1, 1, rows], a_s[TOP, rows], halo[1, 0, rows])
        div[0, rows] = div[0, rows] - use_lo * lo
        div[TOP, rows] = div[TOP, rows] + use_hi * hi
        return 0

    lax.fori_loop(0, NY // 8, edges, 0)

    home = [strip(fro(dx, dy)) for dx, dy in everyone]

    def finish(layer, _):
        for k, rows in enumerate(home):
            res[0, layer, rows] = div[layer, rows] + back[layer, k]
        return 0

    def finish_part(part, first, count):
        theirs = back.at[pl.ds(first, count), pl.ds(0, 7)]
        all_of(theirs, p2_recv.at[part])
        lax.fori_loop(first, first + count, finish, 0)

    finish_part(0, *PARTS[0])

    for part in range(1, n_parts):
        finish_part(part, *PARTS[part])
    finish_part(part_top, TOP, 1)

    @pl.when(lent)
    def _():
        all_of(back.at[0], p2_recv.at[part_first])

    @pl.when(own_first)
    def _():
        all_of(back.at[0, pl.ds(0, 7)], p2_recv.at[part_first])

    finish(0, 0)

    pltpu.make_async_copy(far, far, l2_recv).wait()
    whole = tile[1]
    for dz in range(1, n_z):
        whole = whole + far[dz - 1]
    lane128 = lax.broadcasted_iota(jnp.int32, (8, 128), 1)
    for e in range(2):
        one = jnp.sum(jnp.where(lane128 == slab * 2 + e, whole, 0.0), axis=1, keepdims=True)
        owned[0, :, e:e + 1] = one[:2]

    all_of(got.at[pl.ds(1, CV - 1)], p1_send)
    all_of(ret.at[pl.ds(1, CV - 1)], p2_send)

    @pl.when(own_first)
    def _():
        all_of(got.at[pl.ds(0, 2)], first_send)

    @pl.when(lent)
    def _():
        all_of(j_got, j_send)

    @pl.when(joint)
    def _():
        all_of(w_got, w_send)
        all_of(j_ret, r_send)

    pltpu.make_async_copy(near, near, l1_send).wait()
    pltpu.make_async_copy(far, far, l2_send).wait()


def on_device(*args):
    hbm, vmem = pl.BlockSpec(memory_space=pltpu.HBM), pl.BlockSpec(memory_space=pltpu.VMEM)
    block = (CV, NY, NX)
    dma = pltpu.SemaphoreType.DMA
    return pl.pallas_call(
        kernel,
        out_shape=(jax.ShapeDtypeStruct((1,) + block, F32), jax.ShapeDtypeStruct((1, 2, 2), F32)),
        in_specs=[hbm] * 6,
        out_specs=(vmem, vmem),
        scratch_shapes=[
            pltpu.VMEM(block, F32), pltpu.VMEM(block, F32), pltpu.VMEM(block, F32), pltpu.VMEM(block, F32),
            pltpu.VMEM(block, jnp.int32), pltpu.VMEM(block, jnp.int32),
            pltpu.VMEM((CV, 7, STRIP, NX), F32),
            pltpu.VMEM((CV, 7, STRIP, NX), F32),
            pltpu.VMEM((CV, 8, STRIP, NX), F32),
            pltpu.VMEM((7, STRIP, NX), F32), pltpu.VMEM((2, 8, STRIP, NX), F32), pltpu.VMEM((8, STRIP, NX), F32),
            pltpu.VMEM(block, F32),
            pltpu.VMEM((NY, NX), F32),
            pltpu.VMEM((2, 2, NY, NX), F32),
            pltpu.VMEM((2, 8, 128), F32), pltpu.VMEM((3, 8, 128), F32), pltpu.VMEM((N_SLAB // 4 - 1, 8, 128), F32),
            dma((6,)), dma, dma((len(PARTS) + 2,)), dma, dma((len(PARTS) + 2,)), dma, dma, dma, dma, dma, dma,
            dma((2,)), dma((2,)),
            dma, dma, dma, dma, pltpu.SemaphoreType.REGULAR((2,)),
        ],
        compiler_params=pltpu.CompilerParams(
            collective_id=0, has_side_effects=True, vmem_limit_bytes=52 << 20
        ),
        cost_estimate=pl.CostEstimate(flops=20_000_000, bytes_accessed=8 << 20, transcendentals=0),
    )(*args)


def solution(mesh):
    placed = (
        P("inst", "slab", None, None),
        P("inst", "slab", None, None),
        P("inst", "slab", None, None),
        P("inst", "slab", None, None),
        P("inst", "slab", None, None),
        P("slab", None, None),
    )
    return jax.shard_map(
        on_device,
        mesh=mesh,
        in_specs=placed,
        out_specs=(P("inst", "slab", None, None), P("inst", None, "slab")),
        check_vma=False,
    )
```

```python
import functools
import math

import jax
import jax.numpy as jnp
from jax import lax
from jax.experimental import pallas as pl
from jax.experimental.pallas import tpu as pltpu
from jax.sharding import PartitionSpec as P

MESH = pl.DeviceIdType.MESH
F32 = jnp.float32

GRAVITY = 4.0
SIGMA = 1.0
ROOT2 = math.sqrt(2.0)

CV, NY, NX = 8, 64, 512
N_INST, N_SLAB = 8, 32
NSEC = 64
STRIP = NY // N_INST
PARTS = ((1, 3), (4, 3))
TOP = CV - 1

PEERS = ((1, 0), (0, 1), (1, 1), (0, 3), (1, 3), (0, 2), (1, 2))
GROUP = ((0, 1), (1, 0), (1, 1))


def flux(speed_lo, speed_hi, lower, upper):
    f = 0.5 * (speed_lo + speed_hi)
    return jnp.maximum(f, 0.0) * lower + jnp.minimum(f, 0.0) * upper


def kernel(vf, vu, vv, vw, wet, sec, res, owned,
           a_s, u_s, v_s, w_s, m_s, s_s, got, ret, back, w_got, j_got, j_ret, relay, relay_f, div, plane, halo, tile, near, far,
           in_sem, p1_send, p1_recv, p2_send, p2_recv, first_send, w_send, w_recv, j_send, j_recv, f_send, f_recv, r_send,
           h_send, h_recv, l1_send, l1_recv, l2_send, l2_recv, word):
    inst = lax.axis_index("inst")
    slab = lax.axis_index("slab")
    xh, y = inst // 4, lax.rem(inst, 4)
    zpos, xl, core = slab // 4, lax.rem(slab // 2, 2), lax.rem(slab, 2)

    def to(dx, dy):
        return lax.rem(xh + dx, 2) * 4 + lax.rem(y + dy, 4)

    def fro(dx, dy):
        return lax.rem(xh + dx, 2) * 4 + lax.rem(y + 4 - dy, 4)

    def zto(dz):
        return lax.rem(zpos + dz, n_z) * 4 + xl * 2 + core

    def grp(dxl, dc):
        return zpos * 4 + lax.rem(xl + dxl, 2) * 2 + lax.rem(core + dc, 2)

    n_z = N_SLAB // 4
    zline = ((zpos < n_z - 1, slab + 4), (zpos > 0, slab - 4))
    across = slab + 2 * core - 1
    paired = jnp.logical_and(across >= 0, across < N_SLAB)
    joint = jnp.logical_and(core == 1, paired)
    lent = jnp.logical_and(core == 0, paired)
    own_first = jnp.logical_not(lent)
    flat = core != xl

    barrier = pltpu.get_barrier_semaphore()
    greeted = [(fro(dx, dy), slab) for dx, dy in PEERS]
    greeted += [(inst, grp(a, b)) for a, b in GROUP]
    expected = len(greeted)
    for who in greeted:
        pl.semaphore_signal(barrier, inc=1, device_id=who, device_id_type=MESH)
    for there, who in zline:
        expected = expected + there.astype(jnp.int32)

        @pl.when(there)
        def _():
            pl.semaphore_signal(barrier, inc=1, device_id=(inst, who), device_id_type=MESH)

    expected = expected + N_INST * paired.astype(jnp.int32)

    @pl.when(paired)
    def _():
        for n in range(N_INST):
            pl.semaphore_signal(barrier, inc=1, device_id=(n, across), device_id_type=MESH)

    loads = [
        pltpu.make_async_copy(src.at[0], dst, in_sem.at[i])
        for i, (src, dst) in enumerate(((vf, a_s), (vu, u_s), (vv, v_s), (vw, w_s), (wet, m_s)))
    ]
    loads.append(pltpu.make_async_copy(sec, s_s, in_sem.at[5]))
    for cp in loads:
        cp.start()
    pl.semaphore_wait(barrier, expected)

    def remote(src, dst, send, recv, where):
        return pltpu.make_async_remote_copy(
            src_ref=src, dst_ref=dst, send_sem=send, recv_sem=recv, device_id=where, device_id_type=MESH
        )

    def strip(n):
        return pl.ds(pl.multiple_of(n * STRIP, STRIP), STRIP)

    def send_out(part, first, count):
        layers = pl.ds(first, count)
        for k, (dx, dy) in enumerate(PEERS):
            peer = to(dx, dy)
            remote(vf.at[0, layers, strip(peer)], got.at[layers, k], p1_send, p1_recv.at[part], (peer, slab)).start()

    n_parts = len(PARTS)
    part_top, part_first = n_parts, n_parts + 1
    everyone = PEERS + ((0, 0),)
    slot = {p: k for k, p in enumerate(everyone)}

    half = pl.ds(pl.multiple_of((1 - xh) * (NY // 2), NY // 2), NY // 2)
    same_half = ((0, 0), (0, 1), (0, 3), (0, 2))

    other_half = tuple((1, k) for k in range(4))

    def lend(pairs):
        for dx, dy in pairs:
            peer = to(dx, dy)
            for q, src in enumerate((vf, vw)):
                remote(src.at[0, 0, strip(peer)], j_got.at[q, slot[(dx, dy)]], j_send, j_recv, (peer, across)).start()

    @pl.when(jnp.logical_and(lent, flat))
    def _():
        for q, src in enumerate((vf, vw)):
            remote(src.at[0, 0, half], relay.at[q], j_send, f_recv, (inst, across)).start()

    @pl.when(jnp.logical_and(lent, jnp.logical_not(flat)))
    def _():
        lend(other_half)

    @pl.when(lent)
    def _():
        lend(same_half)

    send_out(0, *PARTS[0])
    send_out(part_top, TOP, 1)

    def send_w(pairs, n):
        for k, (dx, dy) in enumerate(pairs):
            peer = to(dx, dy)
            remote(vw.at[0, TOP, strip(peer)], w_got.at[3 * n + k], w_send.at[n], w_recv.at[n], (peer, slab)).start()

    @pl.when(joint)
    def _():
        send_w(same_half[1:], 0)

    @pl.when(jnp.logical_and(joint, jnp.logical_not(flat)))
    def _():
        send_w(other_half, 1)

    @pl.when(jnp.logical_not(joint))
    def _():
        w_got[0:3] = jnp.zeros((3, STRIP, NX), F32)
        j_got[...] = jnp.zeros_like(j_got)

    @pl.when(jnp.logical_or(jnp.logical_not(joint), flat))
    def _():
        w_got[3:7] = jnp.zeros((4, STRIP, NX), F32)

    def pass_word(way):
        @pl.when(zline[1 - way][0])
        def _():
            pl.semaphore_wait(word.at[way], 1)

        @pl.when(zline[way][0])
        def _():
            pl.semaphore_signal(word.at[way], inc=1, device_id=(inst, zline[way][1]), device_id_type=MESH)

    def spread():
        for dz in range(1, n_z):
            pltpu.make_async_remote_copy(
                src_ref=tile.at[1], dst_ref=far.at[dz - 1], send_sem=l2_send, recv_sem=l2_recv,
                device_id=(inst, zto(dz)), device_id_type=MESH,
            ).start()

    pass_word(0)

    @pl.when(zpos >= n_z // 2)
    def _():
        pass_word(1)

    for cp in loads:
        cp.wait()

    lane = lax.broadcasted_iota(jnp.int32, (8, NX), 1)
    sub = lax.broadcasted_iota(jnp.int32, (8, NX), 0)
    base = lane // (NX // NSEC)
    total = N_SLAB * CV

    def load_rows(r, sums):
        rows = pl.ds(pl.multiple_of(r * 8, 8), 8)

        def load_layer(v, acc):
            u, vy, w = u_s[v, rows], v_s[v, rows], w_s[v, rows]
            depth = ((slab * CV + v).astype(F32) + 0.5) * (GRAVITY / total)
            pressure = depth + 0.5 * (u * u + vy * vy + w * w)
            load = m_s[v, rows].astype(F32) * a_s[v, rows] * pressure
            rel = s_s[v, rows] - base
            return tuple(a + jnp.where(rel == o, load, 0.0) for a, o in zip(acc, (-1, 0, 1)))

        acc = lax.fori_loop(0, CV, load_layer, (jnp.zeros((8, NX), F32),) * 3)
        lever = ((r * 8 + sub).astype(F32) + 0.5) * (1.0 / NY)
        return tuple(s + a for s, a in zip(sums[:3], acc)) + tuple(s + a * lever for s, a in zip(sums[3:], acc))

    sums = lax.fori_loop(0, NY // 8, load_rows, (jnp.zeros((8, NX), F32),) * 6)
    term = jnp.zeros((16, 128), F32)
    col = lax.broadcasted_iota(jnp.int32, (NX, 128), 0) // (NX // NSEC)
    secs = lax.broadcasted_iota(jnp.int32, (NX, 128), 1)
    for n, o in enumerate((-1, 0, 1)):
        pick = (col + o == secs).astype(F32)
        both = jnp.concatenate([sums[n], sums[3 + n]], axis=0)
        term = term + jnp.dot(both, pick, precision=lax.Precision.HIGHEST, preferred_element_type=F32)
    force = jnp.sum(term[:8], axis=0, keepdims=True)
    moment = jnp.sum(term[8:], axis=0, keepdims=True)
    sub128 = lax.broadcasted_iota(jnp.int32, (8, 128), 0)
    tile[0] = jnp.where(sub128 == 0, force, jnp.where(sub128 == 1, moment, 0.0)) * (2.0 / (CV * NY * NX))
    for k, (a, b) in enumerate(GROUP):
        pltpu.make_async_remote_copy(
            src_ref=tile.at[0], dst_ref=near.at[k], send_sem=l1_send, recv_sem=l1_recv,
            device_id=(inst, grp(a, b)), device_id_type=MESH,
        ).start()

    @pl.when(jnp.logical_and(joint, flat))
    def _():
        pltpu.make_async_copy(relay, relay, f_recv).wait()
        relay_f[...] = flux(w_s[TOP, half], relay[1], a_s[TOP, half], relay[0])
        for k in range(4):
            peer = to(1, k)
            rows = strip(lax.rem(peer, 4))
            for q, src in enumerate((relay.at[0], relay_f)):
                remote(src.at[rows], j_got.at[q, slot[(1, k)]], f_send, j_recv, (peer, slab)).start()

    @pl.when(own_first)
    def _():
        for k, (dx, dy) in enumerate(PEERS):
            peer = to(dx, dy)
            remote(vf.at[0, 0, strip(peer)], got.at[0, k], first_send, p1_recv.at[part_first], (peer, slab)).start()

    for part in range(1, n_parts):
        send_out(part, *PARTS[part])

    inner_layer = TOP - TOP * core
    halo_cps = [
        remote(src.at[0, inner_layer], halo.at[core, q], h_send.at[q], h_recv.at[q], (inst, slab + 1 - 2 * core))
        for q, src in enumerate((vf, vw))
    ]
    for cp in halo_cps:
        cp.start()
    halo[core] = jnp.zeros((2, NY, NX), F32)

    plane[...] = jnp.zeros_like(plane)
    first_lane, last_lane = lane == 0, lane == NX - 1
    first_sub, last_sub = sub == 0, sub == 7

    def one_layer(v, _):
        above = jnp.minimum(v + 1, CV - 1)
        inner = jnp.where(v < CV - 1, 1.0, 0.0)
        prev = None
        for r in range(NY // 8):
            rows = pl.ds(r * 8, 8)
            a, u, s, w = a_s[v, rows], u_s[v, rows], v_s[v, rows], w_s[v, rows]
            top = flux(w, w_s[above, rows], a, a_s[above, rows]) * inner
            d = top - plane[rows]
            plane[rows] = top
            if r < NY // 8 - 1:
                nxt = pl.ds(r * 8 + 8, 8)
                a_n, s_n = pltpu.roll(a_s[v, nxt], 7, 0), pltpu.roll(v_s[v, nxt], 7, 0)
            else:
                a_n = s_n = jnp.zeros((8, NX), F32)
            a_up = jnp.where(last_sub, a_n, pltpu.roll(a, 7, 0))
            s_up = jnp.where(last_sub, s_n, pltpu.roll(s, 7, 0))
            fy = flux(s, s_up, a, a_up)
            fy_roll = pltpu.roll(fy, 1, 0)
            if prev is None:
                low = jnp.minimum(0.5 * s, 0.0) * a
            else:
                low = prev
            d = d + (fy - jnp.where(first_sub, low, fy_roll))
            prev = fy_roll
            a_r = jnp.where(last_lane, 0.0, pltpu.roll(a, NX - 1, 1))
            u_r = jnp.where(last_lane, 0.0, pltpu.roll(u, NX - 1, 1))
            fx = flux(u, u_r, a, a_r)
            left = jnp.minimum(0.5 * u, 0.0) * a
            d = d + (fx - jnp.where(first_lane, left, pltpu.roll(fx, 1, 1)))
            div[v, rows] = d
        return 0

    lax.fori_loop(0, CV, one_layer, 0)

    pltpu.make_async_copy(near, near, l1_recv).wait()
    tile[1] = tile[0] + near[0] + near[1] + near[2]

    @pl.when(zpos >= n_z // 2)
    def _():
        spread()

    sig = [jnp.where(y >= k, 1.0, -1.0) for k in range(4)]
    tau = [jnp.where(y + k < 4, 0.5, -0.5) for k in range(4)]
    mine = strip(inst)

    def circulant(value):
        p = [value(0, k) + value(1, k) for k in range(4)]
        q = [(value(0, k) - value(1, k)) * sig[k] for k in range(4)]
        half_odd, half_even = 0.5 * (p[3] - p[1]), 0.5 * (p[0] - p[2])
        nyq = ((p[0] + p[2]) - (p[1] + p[3])) * (SIGMA / N_INST)
        ps = (half_odd + nyq, -half_even - nyq, nyq - half_odd, half_even - nyq)
        qs = (
            q[2] - ROOT2 * (q[1] + q[3]),
            q[1] - ROOT2 * (q[0] + q[2]),
            q[0] - ROOT2 * (q[1] - q[3]),
            -q[3] - ROOT2 * (q[0] - q[2]),
        )
        out = {}
        for t in range(4):
            qt = qs[t] * tau[t]
            out[(0, t)] = ps[t] + qt
            out[(1, t)] = ps[t] - qt
        return out

    halves = [pl.ds(h * 256, 256) for h in range(2)]

    def arrived(layer, cols):
        def value(e, k):
            if (e, k) == (0, 0):
                return a_s[layer, mine, cols]
            return got[layer, slot[(e, k)], :, cols]

        return value

    def put(layer, cols, out):
        for p, value in out.items():
            if p == (0, 0):
                back[layer, 7, :, cols] = value
            else:
                ret[layer, slot[p], :, cols] = value

    def all_of(ref, sem):
        pltpu.make_async_copy(ref, ref, sem).wait()

    def one_strip(layer, _):
        for cols in halves:
            put(layer, cols, circulant(arrived(layer, cols)))
        return 0

    def send_back(part, first, count, send):
        layers = pl.ds(first, count)
        for k, (dx, dy) in enumerate(PEERS):
            remote(ret.at[layers, k], back.at[layers, k], send, p2_recv.at[part], (to(dx, dy), slab)).start()

    def combine(part, first, count):
        all_of(got.at[pl.ds(first, count)], p1_recv.at[part])
        lax.fori_loop(first, first + count, one_strip, 0)
        send_back(part, first, count, p2_send)

    def combine_top():
        all_of(got.at[TOP], p1_recv.at[part_top])

        @pl.when(joint)
        def _():
            all_of(w_got.at[pl.ds(0, 3)], w_recv.at[0])
            all_of(j_got, j_recv)

        @pl.when(jnp.logical_and(joint, jnp.logical_not(flat)))
        def _():
            all_of(w_got.at[pl.ds(3, 4)], w_recv.at[1])

        use = jnp.where(joint, 1.0, 0.0)
        for cols in halves:
            alpha = arrived(TOP, cols)
            face = {}
            for e, k in everyone:
                n = slot[(e, k)]
                if n == 7:
                    w = w_s[TOP, mine, cols]
                else:
                    w = w_got[3 + k if e else same_half.index((e, k)) - 1, :, cols]
                f = flux(w, j_got[1, n, :, cols], alpha(e, k), j_got[0, n, :, cols])
                if e:
                    f = jnp.where(flat, j_got[1, n, :, cols], f)
                face[(e, (4 - k) % 4)] = use * f
            out = circulant(alpha)
            put(TOP, cols, {p: out[p] + face[p] for p in out})
            out = circulant(lambda e, k: j_got[0, slot[(e, k)], :, cols])
            for p in out:
                j_ret[slot[p], :, cols] = out[p] - face[p]
        send_back(part_top, TOP, 1, p2_send)

        @pl.when(joint)
        def _():
            for k, (dx, dy) in enumerate(everyone):
                remote(j_ret.at[k], back.at[0, k], r_send, p2_recv.at[part_first], (to(dx, dy), across)).start()

    combine(0, *PARTS[0])

    @pl.when(own_first)
    def _():
        all_of(got.at[0], p1_recv.at[part_first])
        one_strip(0, 0)
        send_back(part_first, 0, 1, first_send)

    for part in range(1, n_parts):
        combine(part, *PARTS[part])
    combine_top()

    @pl.when(zpos < n_z // 2)
    def _():
        pass_word(1)
        spread()


    for cp in halo_cps:
        cp.wait()
    use_lo = jnp.where(jnp.logical_or(core == 1, slab == 0), 1.0, 0.0)
    use_hi = jnp.where(jnp.logical_or(core == 0, slab == N_SLAB - 1), 1.0, 0.0)

    def edges(r, _):
        rows = pl.ds(pl.multiple_of(r * 8, 8), 8)
        lo = flux(halo[0, 1, rows], w_s[0, rows], halo[0, 0, rows], a_s[0, rows])
        hi = flux(w_s[TOP, rows], halo[1, 1, rows], a_s[TOP, rows], halo[1, 0, rows])
        div[0, rows] = div[0, rows] - use_lo * lo
        div[TOP, rows] = div[TOP, rows] + use_hi * hi
        return 0

    lax.fori_loop(0, NY // 8, edges, 0)

    home = [strip(fro(dx, dy)) for dx, dy in everyone]

    def finish(layer, _):
        for k, rows in enumerate(home):
            res[0, layer, rows] = div[layer, rows] + back[layer, k]
        return 0

    def finish_part(part, first, count):
        theirs = back.at[pl.ds(first, count), pl.ds(0, 7)]
        all_of(theirs, p2_recv.at[part])
        lax.fori_loop(first, first + count, finish, 0)

    finish_part(0, *PARTS[0])

    for part in range(1, n_parts):
        finish_part(part, *PARTS[part])
    finish_part(part_top, TOP, 1)

    @pl.when(lent)
    def _():
        all_of(back.at[0], p2_recv.at[part_first])

    @pl.when(own_first)
    def _():
        all_of(back.at[0, pl.ds(0, 7)], p2_recv.at[part_first])

    finish(0, 0)

    pltpu.make_async_copy(far, far, l2_recv).wait()
    whole = tile[1]
    for dz in range(1, n_z):
        whole = whole + far[dz - 1]
    lane128 = lax.broadcasted_iota(jnp.int32, (8, 128), 1)
    for e in range(2):
        one = jnp.sum(jnp.where(lane128 == slab * 2 + e, whole, 0.0), axis=1, keepdims=True)
        owned[0, :, e:e + 1] = one[:2]

    all_of(got.at[pl.ds(1, CV - 1)], p1_send)
    all_of(ret.at[pl.ds(1, CV - 1)], p2_send)

    @pl.when(own_first)
    def _():
        all_of(got.at[pl.ds(0, 2)], first_send)

    @pl.when(lent)
    def _():
        all_of(j_got, j_send)

    @pl.when(joint)
    def _():
        all_of(w_got.at[pl.ds(0, 3)], w_send.at[0])
        all_of(j_ret, r_send)

    @pl.when(jnp.logical_and(joint, flat))
    def _():
        all_of(j_ret, f_send)

    @pl.when(jnp.logical_and(joint, jnp.logical_not(flat)))
    def _():
        all_of(w_got.at[pl.ds(3, 4)], w_send.at[1])

    pltpu.make_async_copy(near, near, l1_send).wait()
    pltpu.make_async_copy(far, far, l2_send).wait()


def on_device(*args):
    hbm, vmem = pl.BlockSpec(memory_space=pltpu.HBM), pl.BlockSpec(memory_space=pltpu.VMEM)
    block = (CV, NY, NX)
    dma = pltpu.SemaphoreType.DMA
    return pl.pallas_call(
        kernel,
        out_shape=(jax.ShapeDtypeStruct((1,) + block, F32), jax.ShapeDtypeStruct((1, 2, 2), F32)),
        in_specs=[hbm] * 6,
        out_specs=(vmem, vmem),
        scratch_shapes=[
            pltpu.VMEM(block, F32), pltpu.VMEM(block, F32), pltpu.VMEM(block, F32), pltpu.VMEM(block, F32),
            pltpu.VMEM(block, jnp.int32), pltpu.VMEM(block, jnp.int32),
            pltpu.VMEM((CV, 7, STRIP, NX), F32),
            pltpu.VMEM((CV, 7, STRIP, NX), F32),
            pltpu.VMEM((CV, 8, STRIP, NX), F32),
            pltpu.VMEM((7, STRIP, NX), F32), pltpu.VMEM((2, 8, STRIP, NX), F32), pltpu.VMEM((8, STRIP, NX), F32),
            pltpu.VMEM((2, NY // 2, NX), F32), pltpu.VMEM((NY // 2, NX), F32),
            pltpu.VMEM(block, F32),
            pltpu.VMEM((NY, NX), F32),
            pltpu.VMEM((2, 2, NY, NX), F32),
            pltpu.VMEM((2, 8, 128), F32), pltpu.VMEM((3, 8, 128), F32), pltpu.VMEM((N_SLAB // 4 - 1, 8, 128), F32),
            dma((6,)), dma, dma((len(PARTS) + 2,)), dma, dma((len(PARTS) + 2,)), dma, dma((2,)), dma((2,)), dma, dma, dma, dma, dma,
            dma((2,)), dma((2,)),
            dma, dma, dma, dma, pltpu.SemaphoreType.REGULAR((2,)),
        ],
        compiler_params=pltpu.CompilerParams(
            collective_id=0, has_side_effects=True, vmem_limit_bytes=52 << 20
        ),
        cost_estimate=pl.CostEstimate(flops=20_000_000, bytes_accessed=8 << 20, transcendentals=0),
    )(*args)


def solution(mesh):
    placed = (
        P("inst", "slab", None, None),
        P("inst", "slab", None, None),
        P("inst", "slab", None, None),
        P("inst", "slab", None, None),
        P("inst", "slab", None, None),
        P("slab", None, None),
    )
    return jax.shard_map(
        on_device,
        mesh=mesh,
        in_specs=placed,
        out_specs=(P("inst", "slab", None, None), P("inst", None, "slab")),
        check_vma=False,
    )
```

```python
import functools
import math

import jax
import jax.numpy as jnp
from jax import lax
from jax.experimental import pallas as pl
from jax.experimental.pallas import tpu as pltpu
from jax.sharding import PartitionSpec as P

MESH = pl.DeviceIdType.MESH
F32 = jnp.float32

GRAVITY = 4.0
SIGMA = 1.0
ROOT2 = math.sqrt(2.0)

CV, NY, NX = 8, 64, 512
N_INST, N_SLAB = 8, 32
NSEC = 64
STRIP = NY // N_INST
PARTS = ((1, 3), (4, 3))
TOP = CV - 1

PEERS = ((1, 2), (1, 1), (1, 3), (1, 0), (0, 2), (0, 1), (0, 3))
GROUP = ((0, 1), (1, 0), (1, 1))


def flux(speed_lo, speed_hi, lower, upper):
    f = 0.5 * (speed_lo + speed_hi)
    return jnp.maximum(f, 0.0) * lower + jnp.minimum(f, 0.0) * upper


def kernel(vf, vu, vv, vw, wet, sec, res, owned,
           a_s, u_s, v_s, w_s, m_s, s_s, got, ret, back, w_got, j_got, j_ret, relay, relay_f, div, plane, halo, tile, near, far,
           in_sem, p1_send, p1_recv, p2_send, p2_recv, first_send, w_send, w_recv, j_send, j_recv, f_send, f_recv, r_send,
           h_send, h_recv, l1_send, l1_recv, l2_send, l2_recv, word):
    inst = lax.axis_index("inst")
    slab = lax.axis_index("slab")
    xh, y = inst // 4, lax.rem(inst, 4)
    zpos, xl, core = slab // 4, lax.rem(slab // 2, 2), lax.rem(slab, 2)

    def to(dx, dy):
        return lax.rem(xh + dx, 2) * 4 + lax.rem(y + dy, 4)

    def fro(dx, dy):
        return lax.rem(xh + dx, 2) * 4 + lax.rem(y + 4 - dy, 4)

    def zto(dz):
        return lax.rem(zpos + dz, n_z) * 4 + xl * 2 + core

    def grp(dxl, dc):
        return zpos * 4 + lax.rem(xl + dxl, 2) * 2 + lax.rem(core + dc, 2)

    n_z = N_SLAB // 4
    zline = ((zpos < n_z - 1, slab + 4), (zpos > 0, slab - 4))
    across = slab + 2 * core - 1
    paired = jnp.logical_and(across >= 0, across < N_SLAB)
    joint = jnp.logical_and(core == 1, paired)
    lent = jnp.logical_and(core == 0, paired)
    own_first = jnp.logical_not(lent)
    flat = core != xl

    barrier = pltpu.get_barrier_semaphore()
    greeted = [(fro(dx, dy), slab) for dx, dy in PEERS]
    greeted += [(inst, grp(a, b)) for a, b in GROUP]
    expected = len(greeted)
    for who in greeted:
        pl.semaphore_signal(barrier, inc=1, device_id=who, device_id_type=MESH)
    for there, who in zline:
        expected = expected + there.astype(jnp.int32)

        @pl.when(there)
        def _():
            pl.semaphore_signal(barrier, inc=1, device_id=(inst, who), device_id_type=MESH)

    expected = expected + N_INST * paired.astype(jnp.int32)

    @pl.when(paired)
    def _():
        for n in range(N_INST):
            pl.semaphore_signal(barrier, inc=1, device_id=(n, across), device_id_type=MESH)

    loads = [
        pltpu.make_async_copy(src.at[0], dst, in_sem.at[i])
        for i, (src, dst) in enumerate(((vf, a_s), (vu, u_s), (vv, v_s), (vw, w_s), (wet, m_s)))
    ]
    loads.append(pltpu.make_async_copy(sec, s_s, in_sem.at[5]))
    for cp in loads:
        cp.start()
    pl.semaphore_wait(barrier, expected)

    def remote(src, dst, send, recv, where):
        return pltpu.make_async_remote_copy(
            src_ref=src, dst_ref=dst, send_sem=send, recv_sem=recv, device_id=where, device_id_type=MESH
        )

    def strip(n):
        return pl.ds(pl.multiple_of(n * STRIP, STRIP), STRIP)

    def send_out(part, first, count):
        layers = pl.ds(first, count)
        for k, (dx, dy) in enumerate(PEERS):
            peer = to(dx, dy)
            remote(vf.at[0, layers, strip(peer)], got.at[layers, k], p1_send, p1_recv.at[part], (peer, slab)).start()

    n_parts = len(PARTS)
    part_top, part_first = n_parts, n_parts + 1
    everyone = PEERS + ((0, 0),)
    slot = {p: k for k, p in enumerate(everyone)}

    half = pl.ds(pl.multiple_of((1 - xh) * (NY // 2), NY // 2), NY // 2)
    same_half = ((0, 0), (0, 1), (0, 3), (0, 2))

    other_half = tuple((1, k) for k in range(4))

    def lend(pairs):
        for dx, dy in pairs:
            peer = to(dx, dy)
            for q, src in enumerate((vf, vw)):
                remote(src.at[0, 0, strip(peer)], j_got.at[q, slot[(dx, dy)]], j_send, j_recv, (peer, across)).start()

    @pl.when(jnp.logical_and(lent, flat))
    def _():
        for q, src in enumerate((vf, vw)):
            remote(src.at[0, 0, half], relay.at[q], j_send, f_recv, (inst, across)).start()

    @pl.when(jnp.logical_and(lent, jnp.logical_not(flat)))
    def _():
        lend(other_half)

    @pl.when(lent)
    def _():
        lend(same_half)

    send_out(0, *PARTS[0])
    send_out(part_top, TOP, 1)

    def send_w(pairs, n):
        for k, (dx, dy) in enumerate(pairs):
            peer = to(dx, dy)
            remote(vw.at[0, TOP, strip(peer)], w_got.at[3 * n + k], w_send.at[n], w_recv.at[n], (peer, slab)).start()

    @pl.when(joint)
    def _():
        send_w(same_half[1:], 0)

    @pl.when(jnp.logical_and(joint, jnp.logical_not(flat)))
    def _():
        send_w(other_half, 1)

    @pl.when(jnp.logical_not(joint))
    def _():
        w_got[0:3] = jnp.zeros((3, STRIP, NX), F32)
        j_got[...] = jnp.zeros_like(j_got)

    @pl.when(jnp.logical_or(jnp.logical_not(joint), flat))
    def _():
        w_got[3:7] = jnp.zeros((4, STRIP, NX), F32)

    def pass_word(way):
        @pl.when(zline[1 - way][0])
        def _():
            pl.semaphore_wait(word.at[way], 1)

        @pl.when(zline[way][0])
        def _():
            pl.semaphore_signal(word.at[way], inc=1, device_id=(inst, zline[way][1]), device_id_type=MESH)

    def spread():
        for dz in range(1, n_z):
            pltpu.make_async_remote_copy(
                src_ref=tile.at[1], dst_ref=far.at[dz - 1], send_sem=l2_send, recv_sem=l2_recv,
                device_id=(inst, zto(dz)), device_id_type=MESH,
            ).start()

    pass_word(0)

    @pl.when(zpos >= n_z // 2)
    def _():
        pass_word(1)

    for cp in loads:
        cp.wait()

    lane = lax.broadcasted_iota(jnp.int32, (8, NX), 1)
    sub = lax.broadcasted_iota(jnp.int32, (8, NX), 0)
    base = lane // (NX // NSEC)
    total = N_SLAB * CV

    def load_rows(r, sums):
        rows = pl.ds(pl.multiple_of(r * 8, 8), 8)

        def load_layer(v, acc):
            u, vy, w = u_s[v, rows], v_s[v, rows], w_s[v, rows]
            depth = ((slab * CV + v).astype(F32) + 0.5) * (GRAVITY / total)
            pressure = depth + 0.5 * (u * u + vy * vy + w * w)
            load = m_s[v, rows].astype(F32) * a_s[v, rows] * pressure
            rel = s_s[v, rows] - base
            return tuple(a + jnp.where(rel == o, load, 0.0) for a, o in zip(acc, (-1, 0, 1)))

        acc = lax.fori_loop(0, CV, load_layer, (jnp.zeros((8, NX), F32),) * 3)
        lever = ((r * 8 + sub).astype(F32) + 0.5) * (1.0 / NY)
        return tuple(s + a for s, a in zip(sums[:3], acc)) + tuple(s + a * lever for s, a in zip(sums[3:], acc))

    sums = lax.fori_loop(0, NY // 8, load_rows, (jnp.zeros((8, NX), F32),) * 6)
    term = jnp.zeros((16, 128), F32)
    col = lax.broadcasted_iota(jnp.int32, (NX, 128), 0) // (NX // NSEC)
    secs = lax.broadcasted_iota(jnp.int32, (NX, 128), 1)
    for n, o in enumerate((-1, 0, 1)):
        pick = (col + o == secs).astype(F32)
        both = jnp.concatenate([sums[n], sums[3 + n]], axis=0)
        term = term + jnp.dot(both, pick, precision=lax.Precision.HIGHEST, preferred_element_type=F32)
    force = jnp.sum(term[:8], axis=0, keepdims=True)
    moment = jnp.sum(term[8:], axis=0, keepdims=True)
    sub128 = lax.broadcasted_iota(jnp.int32, (8, 128), 0)
    tile[0] = jnp.where(sub128 == 0, force, jnp.where(sub128 == 1, moment, 0.0)) * (2.0 / (CV * NY * NX))
    for k, (a, b) in enumerate(GROUP):
        pltpu.make_async_remote_copy(
            src_ref=tile.at[0], dst_ref=near.at[k], send_sem=l1_send, recv_sem=l1_recv,
            device_id=(inst, grp(a, b)), device_id_type=MESH,
        ).start()

    @pl.when(jnp.logical_and(joint, flat))
    def _():
        pltpu.make_async_copy(relay, relay, f_recv).wait()
        relay_f[...] = flux(w_s[TOP, half], relay[1], a_s[TOP, half], relay[0])
        for k in range(4):
            peer = to(1, k)
            rows = strip(lax.rem(peer, 4))
            for q, src in enumerate((relay.at[0], relay_f)):
                remote(src.at[rows], j_got.at[q, slot[(1, k)]], f_send, j_recv, (peer, slab)).start()

    @pl.when(own_first)
    def _():
        for k, (dx, dy) in enumerate(PEERS):
            peer = to(dx, dy)
            remote(vf.at[0, 0, strip(peer)], got.at[0, k], first_send, p1_recv.at[part_first], (peer, slab)).start()

    for part in range(1, n_parts):
        send_out(part, *PARTS[part])

    inner_layer = TOP - TOP * core
    halo_cps = [
        remote(src.at[0, inner_layer], halo.at[core, q], h_send.at[q], h_recv.at[q], (inst, slab + 1 - 2 * core))
        for q, src in enumerate((vf, vw))
    ]
    for cp in halo_cps:
        cp.start()
    halo[core] = jnp.zeros((2, NY, NX), F32)

    plane[...] = jnp.zeros_like(plane)
    first_lane, last_lane = lane == 0, lane == NX - 1
    first_sub, last_sub = sub == 0, sub == 7

    def one_layer(v, _):
        above = jnp.minimum(v + 1, CV - 1)
        inner = jnp.where(v < CV - 1, 1.0, 0.0)
        prev = None
        for r in range(NY // 8):
            rows = pl.ds(r * 8, 8)
            a, u, s, w = a_s[v, rows], u_s[v, rows], v_s[v, rows], w_s[v, rows]
            top = flux(w, w_s[above, rows], a, a_s[above, rows]) * inner
            d = top - plane[rows]
            plane[rows] = top
            if r < NY // 8 - 1:
                nxt = pl.ds(r * 8 + 8, 8)
                a_n, s_n = pltpu.roll(a_s[v, nxt], 7, 0), pltpu.roll(v_s[v, nxt], 7, 0)
            else:
                a_n = s_n = jnp.zeros((8, NX), F32)
            a_up = jnp.where(last_sub, a_n, pltpu.roll(a, 7, 0))
            s_up = jnp.where(last_sub, s_n, pltpu.roll(s, 7, 0))
            fy = flux(s, s_up, a, a_up)
            fy_roll = pltpu.roll(fy, 1, 0)
            if prev is None:
                low = jnp.minimum(0.5 * s, 0.0) * a
            else:
                low = prev
            d = d + (fy - jnp.where(first_sub, low, fy_roll))
            prev = fy_roll
            a_r = jnp.where(last_lane, 0.0, pltpu.roll(a, NX - 1, 1))
            u_r = jnp.where(last_lane, 0.0, pltpu.roll(u, NX - 1, 1))
            fx = flux(u, u_r, a, a_r)
            left = jnp.minimum(0.5 * u, 0.0) * a
            d = d + (fx - jnp.where(first_lane, left, pltpu.roll(fx, 1, 1)))
            div[v, rows] = d
        return 0

    lax.fori_loop(0, CV, one_layer, 0)

    pltpu.make_async_copy(near, near, l1_recv).wait()
    tile[1] = tile[0] + near[0] + near[1] + near[2]

    @pl.when(zpos >= n_z // 2)
    def _():
        spread()

    sig = [jnp.where(y >= k, 1.0, -1.0) for k in range(4)]
    tau = [jnp.where(y + k < 4, 0.5, -0.5) for k in range(4)]
    mine = strip(inst)

    def circulant(value):
        p = [value(0, k) + value(1, k) for k in range(4)]
        q = [(value(0, k) - value(1, k)) * sig[k] for k in range(4)]
        half_odd, half_even = 0.5 * (p[3] - p[1]), 0.5 * (p[0] - p[2])
        nyq = ((p[0] + p[2]) - (p[1] + p[3])) * (SIGMA / N_INST)
        ps = (half_odd + nyq, -half_even - nyq, nyq - half_odd, half_even - nyq)
        qs = (
            q[2] - ROOT2 * (q[1] + q[3]),
            q[1] - ROOT2 * (q[0] + q[2]),
            q[0] - ROOT2 * (q[1] - q[3]),
            -q[3] - ROOT2 * (q[0] - q[2]),
        )
        out = {}
        for t in range(4):
            qt = qs[t] * tau[t]
            out[(0, t)] = ps[t] + qt
            out[(1, t)] = ps[t] - qt
        return out

    halves = [pl.ds(h * 256, 256) for h in range(2)]

    def arrived(layer, cols):
        def value(e, k):
            if (e, k) == (0, 0):
                return a_s[layer, mine, cols]
            return got[layer, slot[(e, k)], :, cols]

        return value

    def put(layer, cols, out):
        for p, value in out.items():
            if p == (0, 0):
                back[layer, 7, :, cols] = value
            else:
                ret[layer, slot[p], :, cols] = value

    def all_of(ref, sem):
        pltpu.make_async_copy(ref, ref, sem).wait()

    def one_strip(layer, _):
        for cols in halves:
            put(layer, cols, circulant(arrived(layer, cols)))
        return 0

    def send_back(part, first, count, send):
        layers = pl.ds(first, count)
        for k, (dx, dy) in enumerate(PEERS):
            remote(ret.at[layers, k], back.at[layers, k], send, p2_recv.at[part], (to(dx, dy), slab)).start()

    def combine(part, first, count):
        all_of(got.at[pl.ds(first, count)], p1_recv.at[part])
        lax.fori_loop(first, first + count, one_strip, 0)
        send_back(part, first, count, p2_send)

    def combine_top():
        all_of(got.at[TOP], p1_recv.at[part_top])

        @pl.when(joint)
        def _():
            all_of(w_got.at[pl.ds(0, 3)], w_recv.at[0])
            all_of(j_got, j_recv)

        @pl.when(jnp.logical_and(joint, jnp.logical_not(flat)))
        def _():
            all_of(w_got.at[pl.ds(3, 4)], w_recv.at[1])

        use = jnp.where(joint, 1.0, 0.0)
        for cols in halves:
            alpha = arrived(TOP, cols)
            face = {}
            for e, k in everyone:
                n = slot[(e, k)]
                if n == 7:
                    w = w_s[TOP, mine, cols]
                else:
                    w = w_got[3 + k if e else same_half.index((e, k)) - 1, :, cols]
                f = flux(w, j_got[1, n, :, cols], alpha(e, k), j_got[0, n, :, cols])
                if e:
                    f = jnp.where(flat, j_got[1, n, :, cols], f)
                face[(e, (4 - k) % 4)] = use * f
            out = circulant(alpha)
            put(TOP, cols, {p: out[p] + face[p] for p in out})
            out = circulant(lambda e, k: j_got[0, slot[(e, k)], :, cols])
            for p in out:
                j_ret[slot[p], :, cols] = out[p] - face[p]
        send_back(part_top, TOP, 1, p2_send)

        @pl.when(joint)
        def _():
            for k, (dx, dy) in enumerate(everyone):
                remote(j_ret.at[k], back.at[0, k], r_send, p2_recv.at[part_first], (to(dx, dy), across)).start()

    combine(0, *PARTS[0])

    @pl.when(own_first)
    def _():
        all_of(got.at[0], p1_recv.at[part_first])
        one_strip(0, 0)
        send_back(part_first, 0, 1, first_send)

    for part in range(1, n_parts):
        combine(part, *PARTS[part])
    combine_top()

    @pl.when(zpos < n_z // 2)
    def _():
        pass_word(1)
        spread()


    for cp in halo_cps:
        cp.wait()
    use_lo = jnp.where(jnp.logical_or(core == 1, slab == 0), 1.0, 0.0)
    use_hi = jnp.where(jnp.logical_or(core == 0, slab == N_SLAB - 1), 1.0, 0.0)

    def edges(r, _):
        rows = pl.ds(pl.multiple_of(r * 8, 8), 8)
        lo = flux(halo[0, 1, rows], w_s[0, rows], halo[0, 0, rows], a_s[0, rows])
        hi = flux(w_s[TOP, rows], halo[1, 1, rows], a_s[TOP, rows], halo[1, 0, rows])
        div[0, rows] = div[0, rows] - use_lo * lo
        div[TOP, rows] = div[TOP, rows] + use_hi * hi
        return 0

    lax.fori_loop(0, NY // 8, edges, 0)

    home = [strip(fro(dx, dy)) for dx, dy in everyone]

    def finish(layer, _):
        for k, rows in enumerate(home):
            res[0, layer, rows] = div[layer, rows] + back[layer, k]
        return 0

    def finish_part(part, first, count):
        theirs = back.at[pl.ds(first, count), pl.ds(0, 7)]
        all_of(theirs, p2_recv.at[part])
        lax.fori_loop(first, first + count, finish, 0)

    finish_part(0, *PARTS[0])

    for part in range(1, n_parts):
        finish_part(part, *PARTS[part])
    finish_part(part_top, TOP, 1)

    @pl.when(lent)
    def _():
        all_of(back.at[0], p2_recv.at[part_first])

    @pl.when(own_first)
    def _():
        all_of(back.at[0, pl.ds(0, 7)], p2_recv.at[part_first])

    finish(0, 0)

    pltpu.make_async_copy(far, far, l2_recv).wait()
    whole = tile[1]
    for dz in range(1, n_z):
        whole = whole + far[dz - 1]
    lane128 = lax.broadcasted_iota(jnp.int32, (8, 128), 1)
    for e in range(2):
        one = jnp.sum(jnp.where(lane128 == slab * 2 + e, whole, 0.0), axis=1, keepdims=True)
        owned[0, :, e:e + 1] = one[:2]

    all_of(got.at[pl.ds(1, CV - 1)], p1_send)
    all_of(ret.at[pl.ds(1, CV - 1)], p2_send)

    @pl.when(own_first)
    def _():
        all_of(got.at[pl.ds(0, 2)], first_send)

    @pl.when(lent)
    def _():
        all_of(j_got, j_send)

    @pl.when(joint)
    def _():
        all_of(w_got.at[pl.ds(0, 3)], w_send.at[0])
        all_of(j_ret, r_send)

    @pl.when(jnp.logical_and(joint, flat))
    def _():
        all_of(j_ret, f_send)

    @pl.when(jnp.logical_and(joint, jnp.logical_not(flat)))
    def _():
        all_of(w_got.at[pl.ds(3, 4)], w_send.at[1])

    pltpu.make_async_copy(near, near, l1_send).wait()
    pltpu.make_async_copy(far, far, l2_send).wait()


def hand_over(res, owned, res_out, owned_out, sem):
    copies = [
        pltpu.make_async_copy(src, dst, sem.at[n]) for n, (src, dst) in enumerate(((res, res_out), (owned, owned_out)))
    ]
    for cp in copies:
        cp.start()
    for cp in copies:
        cp.wait()


def on_device(*args):
    hbm, vmem = pl.BlockSpec(memory_space=pltpu.HBM), pl.BlockSpec(memory_space=pltpu.VMEM)
    block = (CV, NY, NX)
    dma = pltpu.SemaphoreType.DMA
    made = pl.pallas_call(
        kernel,
        out_shape=(jax.ShapeDtypeStruct((1,) + block, F32), jax.ShapeDtypeStruct((1, 2, 2), F32)),
        in_specs=[hbm] * 6,
        out_specs=(vmem, vmem),
        scratch_shapes=[
            pltpu.VMEM(block, F32), pltpu.VMEM(block, F32), pltpu.VMEM(block, F32), pltpu.VMEM(block, F32),
            pltpu.VMEM(block, jnp.int32), pltpu.VMEM(block, jnp.int32),
            pltpu.VMEM((CV, 7, STRIP, NX), F32),
            pltpu.VMEM((CV, 7, STRIP, NX), F32),
            pltpu.VMEM((CV, 8, STRIP, NX), F32),
            pltpu.VMEM((7, STRIP, NX), F32), pltpu.VMEM((2, 8, STRIP, NX), F32), pltpu.VMEM((8, STRIP, NX), F32),
            pltpu.VMEM((2, NY // 2, NX), F32), pltpu.VMEM((NY // 2, NX), F32),
            pltpu.VMEM(block, F32),
            pltpu.VMEM((NY, NX), F32),
            pltpu.VMEM((2, 2, NY, NX), F32),
            pltpu.VMEM((2, 8, 128), F32), pltpu.VMEM((3, 8, 128), F32), pltpu.VMEM((N_SLAB // 4 - 1, 8, 128), F32),
            dma((6,)), dma, dma((len(PARTS) + 2,)), dma, dma((len(PARTS) + 2,)), dma, dma((2,)), dma((2,)), dma, dma, dma, dma, dma,
            dma((2,)), dma((2,)),
            dma, dma, dma, dma, pltpu.SemaphoreType.REGULAR((2,)),
        ],
        compiler_params=pltpu.CompilerParams(
            collective_id=0, has_side_effects=True, vmem_limit_bytes=52 << 20
        ),
        cost_estimate=pl.CostEstimate(flops=20_000_000, bytes_accessed=8 << 20, transcendentals=0),
    )(*args)
    return pl.pallas_call(
        hand_over,
        out_shape=tuple(jax.ShapeDtypeStruct(m.shape, F32) for m in made),
        in_specs=[vmem, vmem],
        out_specs=(hbm, hbm),
        scratch_shapes=[dma((2,))],
        compiler_params=pltpu.CompilerParams(vmem_limit_bytes=1 << 20),
    )(*made)


def solution(mesh):
    placed = (
        P("inst", "slab", None, None),
        P("inst", "slab", None, None),
        P("inst", "slab", None, None),
        P("inst", "slab", None, None),
        P("inst", "slab", None, None),
        P("slab", None, None),
    )
    return jax.shard_map(
        on_device,
        mesh=mesh,
        in_specs=placed,
        out_specs=(P("inst", "slab", None, None), P("inst", None, "slab")),
        check_vma=False,
    )
```

```python
import functools
import math

import jax
import jax.numpy as jnp
from jax import lax
from jax.experimental import pallas as pl
from jax.experimental.pallas import tpu as pltpu
from jax.sharding import PartitionSpec as P

MESH = pl.DeviceIdType.MESH
F32 = jnp.float32

GRAVITY = 4.0
SIGMA = 1.0
ROOT2 = math.sqrt(2.0)

CV, NY, NX = 8, 64, 512
N_INST, N_SLAB = 8, 32
NSEC = 64
STRIP = NY // N_INST
PARTS = ((1, 3), (4, 3))
TOP = CV - 1

PEERS = ((1, 2), (1, 1), (1, 3), (1, 0), (0, 2), (0, 1), (0, 3))
GROUP = ((0, 1), (1, 0), (1, 1))


def flux(speed_lo, speed_hi, lower, upper):
    f = 0.5 * (speed_lo + speed_hi)
    return jnp.maximum(f, 0.0) * lower + jnp.minimum(f, 0.0) * upper


def kernel(vf, vu, vv, vw, wet, sec, res, owned,
           a_s, u_s, v_s, w_s, m_s, s_s, got, ret, back, w_got, j_got, j_ret, relay, relay_f, div, plane, halo, tile, near, far,
           in_sem, p1_send, p1_recv, p2_send, p2_recv, first_send, w_send, w_recv, j_send, j_recv, f_send, f_recv, r_send,
           h_send, h_recv, l1_send, l1_recv, l2_send, l2_recv, word):
    inst = lax.axis_index("inst")
    slab = lax.axis_index("slab")
    xh, y = inst // 4, lax.rem(inst, 4)
    zpos, xl, core = slab // 4, lax.rem(slab // 2, 2), lax.rem(slab, 2)

    def to(dx, dy):
        return lax.rem(xh + dx, 2) * 4 + lax.rem(y + dy, 4)

    def fro(dx, dy):
        return lax.rem(xh + dx, 2) * 4 + lax.rem(y + 4 - dy, 4)

    def zto(dz):
        return lax.rem(zpos + dz, n_z) * 4 + xl * 2 + core

    def grp(dxl, dc):
        return zpos * 4 + lax.rem(xl + dxl, 2) * 2 + lax.rem(core + dc, 2)

    n_z = N_SLAB // 4
    zline = ((zpos < n_z - 1, slab + 4), (zpos > 0, slab - 4))
    across = slab + 2 * core - 1
    paired = jnp.logical_and(across >= 0, across < N_SLAB)
    joint = jnp.logical_and(core == 1, paired)
    lent = jnp.logical_and(core == 0, paired)
    own_first = jnp.logical_not(lent)
    flat = core != xl

    barrier = pltpu.get_barrier_semaphore()
    greeted = [(fro(dx, dy), slab) for dx, dy in PEERS]
    greeted += [(inst, grp(a, b)) for a, b in GROUP]
    expected = len(greeted)
    for who in greeted:
        pl.semaphore_signal(barrier, inc=1, device_id=who, device_id_type=MESH)
    for there, who in zline:
        expected = expected + there.astype(jnp.int32)

        @pl.when(there)
        def _():
            pl.semaphore_signal(barrier, inc=1, device_id=(inst, who), device_id_type=MESH)

    expected = expected + N_INST * paired.astype(jnp.int32)

    @pl.when(paired)
    def _():
        for n in range(N_INST):
            pl.semaphore_signal(barrier, inc=1, device_id=(n, across), device_id_type=MESH)

    loads = [
        pltpu.make_async_copy(src.at[0], dst, in_sem.at[i])
        for i, (src, dst) in enumerate(((vf, a_s), (vu, u_s), (vv, v_s), (vw, w_s), (wet, m_s)))
    ]
    loads.append(pltpu.make_async_copy(sec, s_s, in_sem.at[5]))
    for cp in loads:
        cp.start()
    pl.semaphore_wait(barrier, expected)

    def remote(src, dst, send, recv, where):
        return pltpu.make_async_remote_copy(
            src_ref=src, dst_ref=dst, send_sem=send, recv_sem=recv, device_id=where, device_id_type=MESH
        )

    def strip(n):
        return pl.ds(pl.multiple_of(n * STRIP, STRIP), STRIP)

    def send_out(part, first, count):
        layers = pl.ds(first, count)
        for k, (dx, dy) in enumerate(PEERS):
            peer = to(dx, dy)
            remote(vf.at[0, layers, strip(peer)], got.at[layers, k], p1_send, p1_recv.at[part], (peer, slab)).start()

    n_parts = len(PARTS)
    part_top, part_first = n_parts, n_parts + 1
    everyone = PEERS + ((0, 0),)
    slot = {p: k for k, p in enumerate(everyone)}

    half = pl.ds(pl.multiple_of((1 - xh) * (NY // 2), NY // 2), NY // 2)
    same_half = ((0, 0), (0, 1), (0, 3), (0, 2))

    other_half = tuple((1, k) for k in range(4))

    def lend(pairs):
        for dx, dy in pairs:
            peer = to(dx, dy)
            for q, src in enumerate((vf, vw)):
                remote(src.at[0, 0, strip(peer)], j_got.at[q, slot[(dx, dy)]], j_send, j_recv, (peer, across)).start()

    @pl.when(jnp.logical_and(lent, flat))
    def _():
        for q, src in enumerate((vf, vw)):
            remote(src.at[0, 0, half], relay.at[q], j_send, f_recv, (inst, across)).start()

    @pl.when(jnp.logical_and(lent, jnp.logical_not(flat)))
    def _():
        lend(other_half)

    @pl.when(lent)
    def _():
        lend(same_half)

    send_out(0, *PARTS[0])
    send_out(part_top, TOP, 1)

    def send_w(pairs, n):
        for k, (dx, dy) in enumerate(pairs):
            peer = to(dx, dy)
            remote(vw.at[0, TOP, strip(peer)], w_got.at[3 * n + k], w_send.at[n], w_recv.at[n], (peer, slab)).start()

    @pl.when(joint)
    def _():
        send_w(same_half[1:], 0)

    @pl.when(jnp.logical_and(joint, jnp.logical_not(flat)))
    def _():
        send_w(other_half, 1)

    @pl.when(jnp.logical_not(joint))
    def _():
        w_got[0:3] = jnp.zeros((3, STRIP, NX), F32)
        j_got[...] = jnp.zeros_like(j_got)

    @pl.when(jnp.logical_or(jnp.logical_not(joint), flat))
    def _():
        w_got[3:7] = jnp.zeros((4, STRIP, NX), F32)

    def pass_word(way):
        @pl.when(zline[1 - way][0])
        def _():
            pl.semaphore_wait(word.at[way], 1)

        @pl.when(zline[way][0])
        def _():
            pl.semaphore_signal(word.at[way], inc=1, device_id=(inst, zline[way][1]), device_id_type=MESH)

    def spread():
        for dz in range(1, n_z):
            pltpu.make_async_remote_copy(
                src_ref=tile.at[1], dst_ref=far.at[dz - 1], send_sem=l2_send, recv_sem=l2_recv,
                device_id=(inst, zto(dz)), device_id_type=MESH,
            ).start()

    pass_word(0)

    @pl.when(zpos >= n_z // 2)
    def _():
        pass_word(1)

    for cp in loads:
        cp.wait()

    @pl.when(jnp.logical_and(joint, flat))
    def _():
        pltpu.make_async_copy(relay, relay, f_recv).wait()
        relay_f[...] = flux(w_s[TOP, half], relay[1], a_s[TOP, half], relay[0])
        for k in range(4):
            peer = to(1, k)
            rows = strip(lax.rem(peer, 4))
            for q, src in enumerate((relay.at[0], relay_f)):
                remote(src.at[rows], j_got.at[q, slot[(1, k)]], f_send, j_recv, (peer, slab)).start()

    lane = lax.broadcasted_iota(jnp.int32, (8, NX), 1)
    sub = lax.broadcasted_iota(jnp.int32, (8, NX), 0)
    base = lane // (NX // NSEC)
    total = N_SLAB * CV

    def load_rows(r, sums):
        rows = pl.ds(pl.multiple_of(r * 8, 8), 8)

        def load_layer(v, acc):
            u, vy, w = u_s[v, rows], v_s[v, rows], w_s[v, rows]
            depth = ((slab * CV + v).astype(F32) + 0.5) * (GRAVITY / total)
            pressure = depth + 0.5 * (u * u + vy * vy + w * w)
            load = m_s[v, rows].astype(F32) * a_s[v, rows] * pressure
            rel = s_s[v, rows] - base
            return tuple(a + jnp.where(rel == o, load, 0.0) for a, o in zip(acc, (-1, 0, 1)))

        acc = lax.fori_loop(0, CV, load_layer, (jnp.zeros((8, NX), F32),) * 3)
        lever = ((r * 8 + sub).astype(F32) + 0.5) * (1.0 / NY)
        return tuple(s + a for s, a in zip(sums[:3], acc)) + tuple(s + a * lever for s, a in zip(sums[3:], acc))

    sums = lax.fori_loop(0, NY // 8, load_rows, (jnp.zeros((8, NX), F32),) * 6)
    term = jnp.zeros((16, 128), F32)
    col = lax.broadcasted_iota(jnp.int32, (NX, 128), 0) // (NX // NSEC)
    secs = lax.broadcasted_iota(jnp.int32, (NX, 128), 1)
    for n, o in enumerate((-1, 0, 1)):
        pick = (col + o == secs).astype(F32)
        both = jnp.concatenate([sums[n], sums[3 + n]], axis=0)
        term = term + jnp.dot(both, pick, precision=lax.Precision.HIGHEST, preferred_element_type=F32)
    force = jnp.sum(term[:8], axis=0, keepdims=True)
    moment = jnp.sum(term[8:], axis=0, keepdims=True)
    sub128 = lax.broadcasted_iota(jnp.int32, (8, 128), 0)
    tile[0] = jnp.where(sub128 == 0, force, jnp.where(sub128 == 1, moment, 0.0)) * (2.0 / (CV * NY * NX))
    for k, (a, b) in enumerate(GROUP):
        pltpu.make_async_remote_copy(
            src_ref=tile.at[0], dst_ref=near.at[k], send_sem=l1_send, recv_sem=l1_recv,
            device_id=(inst, grp(a, b)), device_id_type=MESH,
        ).start()

    @pl.when(own_first)
    def _():
        for k, (dx, dy) in enumerate(PEERS):
            peer = to(dx, dy)
            remote(vf.at[0, 0, strip(peer)], got.at[0, k], first_send, p1_recv.at[part_first], (peer, slab)).start()

    for part in range(1, n_parts):
        send_out(part, *PARTS[part])

    inner_layer = TOP - TOP * core
    halo_cps = [
        remote(src.at[0, inner_layer], halo.at[core, q], h_send.at[q], h_recv.at[q], (inst, slab + 1 - 2 * core))
        for q, src in enumerate((vf, vw))
    ]
    for cp in halo_cps:
        cp.start()
    halo[core] = jnp.zeros((2, NY, NX), F32)

    plane[...] = jnp.zeros_like(plane)
    first_lane, last_lane = lane == 0, lane == NX - 1
    first_sub, last_sub = sub == 0, sub == 7

    def one_layer(v, _):
        above = jnp.minimum(v + 1, CV - 1)
        inner = jnp.where(v < CV - 1, 1.0, 0.0)
        prev = None
        for r in range(NY // 8):
            rows = pl.ds(r * 8, 8)
            a, u, s, w = a_s[v, rows], u_s[v, rows], v_s[v, rows], w_s[v, rows]
            top = flux(w, w_s[above, rows], a, a_s[above, rows]) * inner
            d = top - plane[rows]
            plane[rows] = top
            if r < NY // 8 - 1:
                nxt = pl.ds(r * 8 + 8, 8)
                a_n, s_n = pltpu.roll(a_s[v, nxt], 7, 0), pltpu.roll(v_s[v, nxt], 7, 0)
            else:
                a_n = s_n = jnp.zeros((8, NX), F32)
            a_up = jnp.where(last_sub, a_n, pltpu.roll(a, 7, 0))
            s_up = jnp.where(last_sub, s_n, pltpu.roll(s, 7, 0))
            fy = flux(s, s_up, a, a_up)
            fy_roll = pltpu.roll(fy, 1, 0)
            if prev is None:
                low = jnp.minimum(0.5 * s, 0.0) * a
            else:
                low = prev
            d = d + (fy - jnp.where(first_sub, low, fy_roll))
            prev = fy_roll
            a_r = jnp.where(last_lane, 0.0, pltpu.roll(a, NX - 1, 1))
            u_r = jnp.where(last_lane, 0.0, pltpu.roll(u, NX - 1, 1))
            fx = flux(u, u_r, a, a_r)
            left = jnp.minimum(0.5 * u, 0.0) * a
            d = d + (fx - jnp.where(first_lane, left, pltpu.roll(fx, 1, 1)))
            div[v, rows] = d
        return 0

    lax.fori_loop(0, CV, one_layer, 0)

    pltpu.make_async_copy(near, near, l1_recv).wait()
    tile[1] = tile[0] + near[0] + near[1] + near[2]

    @pl.when(zpos >= n_z // 2)
    def _():
        spread()

    sig = [jnp.where(y >= k, 1.0, -1.0) for k in range(4)]
    tau = [jnp.where(y + k < 4, 0.5, -0.5) for k in range(4)]
    mine = strip(inst)

    def circulant(value):
        p = [value(0, k) + value(1, k) for k in range(4)]
        q = [(value(0, k) - value(1, k)) * sig[k] for k in range(4)]
        half_odd, half_even = 0.5 * (p[3] - p[1]), 0.5 * (p[0] - p[2])
        nyq = ((p[0] + p[2]) - (p[1] + p[3])) * (SIGMA / N_INST)
        ps = (half_odd + nyq, -half_even - nyq, nyq - half_odd, half_even - nyq)
        qs = (
            q[2] - ROOT2 * (q[1] + q[3]),
            q[1] - ROOT2 * (q[0] + q[2]),
            q[0] - ROOT2 * (q[1] - q[3]),
            -q[3] - ROOT2 * (q[0] - q[2]),
        )
        out = {}
        for t in range(4):
            qt = qs[t] * tau[t]
            out[(0, t)] = ps[t] + qt
            out[(1, t)] = ps[t] - qt
        return out

    halves = [pl.ds(h * 256, 256) for h in range(2)]

    def arrived(layer, cols):
        def value(e, k):
            if (e, k) == (0, 0):
                return a_s[layer, mine, cols]
            return got[layer, slot[(e, k)], :, cols]

        return value

    def put(layer, cols, out):
        for p, value in out.items():
            if p == (0, 0):
                back[layer, 7, :, cols] = value
            else:
                ret[layer, slot[p], :, cols] = value

    def all_of(ref, sem):
        pltpu.make_async_copy(ref, ref, sem).wait()

    def one_strip(layer, _):
        for cols in halves:
            put(layer, cols, circulant(arrived(layer, cols)))
        return 0

    def send_back(part, first, count, send):
        layers = pl.ds(first, count)
        for k, (dx, dy) in enumerate(PEERS):
            remote(ret.at[layers, k], back.at[layers, k], send, p2_recv.at[part], (to(dx, dy), slab)).start()

    def combine(part, first, count):
        all_of(got.at[pl.ds(first, count)], p1_recv.at[part])
        lax.fori_loop(first, first + count, one_strip, 0)
        send_back(part, first, count, p2_send)

    def combine_top():
        all_of(got.at[TOP], p1_recv.at[part_top])

        @pl.when(joint)
        def _():
            all_of(w_got.at[pl.ds(0, 3)], w_recv.at[0])
            all_of(j_got, j_recv)

        @pl.when(jnp.logical_and(joint, jnp.logical_not(flat)))
        def _():
            all_of(w_got.at[pl.ds(3, 4)], w_recv.at[1])

        use = jnp.where(joint, 1.0, 0.0)
        for cols in halves:
            alpha = arrived(TOP, cols)
            face = {}
            for e, k in everyone:
                n = slot[(e, k)]
                if n == 7:
                    w = w_s[TOP, mine, cols]
                else:
                    w = w_got[3 + k if e else same_half.index((e, k)) - 1, :, cols]
                f = flux(w, j_got[1, n, :, cols], alpha(e, k), j_got[0, n, :, cols])
                if e:
                    f = jnp.where(flat, j_got[1, n, :, cols], f)
                face[(e, (4 - k) % 4)] = use * f
            out = circulant(alpha)
            put(TOP, cols, {p: out[p] + face[p] for p in out})
            out = circulant(lambda e, k: j_got[0, slot[(e, k)], :, cols])
            for p in out:
                j_ret[slot[p], :, cols] = out[p] - face[p]
        send_back(part_top, TOP, 1, p2_send)

        @pl.when(joint)
        def _():
            for k, (dx, dy) in enumerate(everyone):
                remote(j_ret.at[k], back.at[0, k], r_send, p2_recv.at[part_first], (to(dx, dy), across)).start()

    combine(0, *PARTS[0])

    @pl.when(own_first)
    def _():
        all_of(got.at[0], p1_recv.at[part_first])
        one_strip(0, 0)
        send_back(part_first, 0, 1, first_send)

    for part in range(1, n_parts):
        combine(part, *PARTS[part])
    combine_top()

    @pl.when(zpos < n_z // 2)
    def _():
        pass_word(1)
        spread()


    for cp in halo_cps:
        cp.wait()
    use_lo = jnp.where(jnp.logical_or(core == 1, slab == 0), 1.0, 0.0)
    use_hi = jnp.where(jnp.logical_or(core == 0, slab == N_SLAB - 1), 1.0, 0.0)

    def edges(r, _):
        rows = pl.ds(pl.multiple_of(r * 8, 8), 8)
        lo = flux(halo[0, 1, rows], w_s[0, rows], halo[0, 0, rows], a_s[0, rows])
        hi = flux(w_s[TOP, rows], halo[1, 1, rows], a_s[TOP, rows], halo[1, 0, rows])
        div[0, rows] = div[0, rows] - use_lo * lo
        div[TOP, rows] = div[TOP, rows] + use_hi * hi
        return 0

    lax.fori_loop(0, NY // 8, edges, 0)

    home = [strip(fro(dx, dy)) for dx, dy in everyone]

    def finish(layer, _):
        for k, rows in enumerate(home):
            res[0, layer, rows] = div[layer, rows] + back[layer, k]
        return 0

    def finish_part(part, first, count):
        theirs = back.at[pl.ds(first, count), pl.ds(0, 7)]
        all_of(theirs, p2_recv.at[part])
        lax.fori_loop(first, first + count, finish, 0)

    finish_part(0, *PARTS[0])

    for part in range(1, n_parts):
        finish_part(part, *PARTS[part])

    pltpu.make_async_copy(far, far, l2_recv).wait()
    whole = tile[1]
    for dz in range(1, n_z):
        whole = whole + far[dz - 1]
    lane128 = lax.broadcasted_iota(jnp.int32, (8, 128), 1)
    for e in range(2):
        one = jnp.sum(jnp.where(lane128 == slab * 2 + e, whole, 0.0), axis=1, keepdims=True)
        owned[0, :, e:e + 1] = one[:2]

    finish_part(part_top, TOP, 1)

    @pl.when(lent)
    def _():
        all_of(back.at[0], p2_recv.at[part_first])

    @pl.when(own_first)
    def _():
        all_of(back.at[0, pl.ds(0, 7)], p2_recv.at[part_first])

    finish(0, 0)

    all_of(got.at[pl.ds(1, CV - 1)], p1_send)
    all_of(ret.at[pl.ds(1, CV - 1)], p2_send)

    @pl.when(own_first)
    def _():
        all_of(got.at[pl.ds(0, 2)], first_send)

    @pl.when(lent)
    def _():
        all_of(j_got, j_send)

    @pl.when(joint)
    def _():
        all_of(w_got.at[pl.ds(0, 3)], w_send.at[0])
        all_of(j_ret, r_send)

    @pl.when(jnp.logical_and(joint, flat))
    def _():
        all_of(j_ret, f_send)

    @pl.when(jnp.logical_and(joint, jnp.logical_not(flat)))
    def _():
        all_of(w_got.at[pl.ds(3, 4)], w_send.at[1])

    pltpu.make_async_copy(near, near, l1_send).wait()
    pltpu.make_async_copy(far, far, l2_send).wait()


def hand_over(res, owned, res_out, owned_out, sem):
    copies = [
        pltpu.make_async_copy(src, dst, sem.at[n]) for n, (src, dst) in enumerate(((res, res_out), (owned, owned_out)))
    ]
    for cp in copies:
        cp.start()
    for cp in copies:
        cp.wait()


def on_device(*args):
    hbm, vmem = pl.BlockSpec(memory_space=pltpu.HBM), pl.BlockSpec(memory_space=pltpu.VMEM)
    block = (CV, NY, NX)
    dma = pltpu.SemaphoreType.DMA
    made = pl.pallas_call(
        kernel,
        out_shape=(jax.ShapeDtypeStruct((1,) + block, F32), jax.ShapeDtypeStruct((1, 2, 2), F32)),
        in_specs=[hbm] * 6,
        out_specs=(vmem, vmem),
        scratch_shapes=[
            pltpu.VMEM(block, F32), pltpu.VMEM(block, F32), pltpu.VMEM(block, F32), pltpu.VMEM(block, F32),
            pltpu.VMEM(block, jnp.int32), pltpu.VMEM(block, jnp.int32),
            pltpu.VMEM((CV, 7, STRIP, NX), F32),
            pltpu.VMEM((CV, 7, STRIP, NX), F32),
            pltpu.VMEM((CV, 8, STRIP, NX), F32),
            pltpu.VMEM((7, STRIP, NX), F32), pltpu.VMEM((2, 8, STRIP, NX), F32), pltpu.VMEM((8, STRIP, NX), F32),
            pltpu.VMEM((2, NY // 2, NX), F32), pltpu.VMEM((NY // 2, NX), F32),
            pltpu.VMEM(block, F32),
            pltpu.VMEM((NY, NX), F32),
            pltpu.VMEM((2, 2, NY, NX), F32),
            pltpu.VMEM((2, 8, 128), F32), pltpu.VMEM((3, 8, 128), F32), pltpu.VMEM((N_SLAB // 4 - 1, 8, 128), F32),
            dma((6,)), dma, dma((len(PARTS) + 2,)), dma, dma((len(PARTS) + 2,)), dma, dma((2,)), dma((2,)), dma, dma, dma, dma, dma,
            dma((2,)), dma((2,)),
            dma, dma, dma, dma, pltpu.SemaphoreType.REGULAR((2,)),
        ],
        compiler_params=pltpu.CompilerParams(
            collective_id=0, has_side_effects=True, vmem_limit_bytes=52 << 20
        ),
        cost_estimate=pl.CostEstimate(flops=20_000_000, bytes_accessed=8 << 20, transcendentals=0),
    )(*args)
    return pl.pallas_call(
        hand_over,
        out_shape=tuple(jax.ShapeDtypeStruct(m.shape, F32) for m in made),
        in_specs=[vmem, vmem],
        out_specs=(hbm, hbm),
        scratch_shapes=[dma((2,))],
        compiler_params=pltpu.CompilerParams(vmem_limit_bytes=1 << 20),
    )(*made)


def solution(mesh):
    placed = (
        P("inst", "slab", None, None),
        P("inst", "slab", None, None),
        P("inst", "slab", None, None),
        P("inst", "slab", None, None),
        P("inst", "slab", None, None),
        P("slab", None, None),
    )
    return jax.shard_map(
        on_device,
        mesh=mesh,
        in_specs=placed,
        out_specs=(P("inst", "slab", None, None), P("inst", None, "slab")),
        check_vma=False,
    )
```

```python
import functools
import math

import jax
import jax.numpy as jnp
from jax import lax
from jax.experimental import pallas as pl
from jax.experimental.pallas import tpu as pltpu
from jax.sharding import PartitionSpec as P

MESH = pl.DeviceIdType.MESH
F32 = jnp.float32

GRAVITY = 4.0
SIGMA = 1.0
ROOT2 = math.sqrt(2.0)

CV, NY, NX = 8, 64, 512
N_INST, N_SLAB = 8, 32
NSEC = 64
STRIP = NY // N_INST
PARTS = ((1, 3), (4, 3))
TOP = CV - 1

PEERS = ((1, 2), (1, 1), (1, 3), (1, 0), (0, 2), (0, 1), (0, 3))
GROUP = ((0, 1), (1, 0), (1, 1))


def flux(speed_lo, speed_hi, lower, upper):
    f = 0.5 * (speed_lo + speed_hi)
    return jnp.maximum(f, 0.0) * lower + jnp.minimum(f, 0.0) * upper


def kernel(vf, vu, vv, vw, wet, sec, res, owned,
           a_s, u_s, v_s, w_s, m_s, s_s, got, ret, back, w_got, j_got, j_ret, relay, relay_f, div, plane, halo, tile, near, far, summed,
           in_sem, p1_send, p1_recv, p2_send, p2_recv, first_send, w_send, w_recv, j_send, j_recv, f_send, f_recv, r_send,
           h_send, h_recv, l1_send, l1_recv, l2_send, l2_recv, t_send, t_recv, word):
    inst = lax.axis_index("inst")
    slab = lax.axis_index("slab")
    xh, y = inst // 4, lax.rem(inst, 4)
    zpos, xl, core = slab // 4, lax.rem(slab // 2, 2), lax.rem(slab, 2)

    def to(dx, dy):
        return lax.rem(xh + dx, 2) * 4 + lax.rem(y + dy, 4)

    def fro(dx, dy):
        return lax.rem(xh + dx, 2) * 4 + lax.rem(y + 4 - dy, 4)

    def zto(dz):
        return lax.rem(zpos + dz, n_z) * 4 + xl * 2 + core

    def grp(dxl, dc):
        return zpos * 4 + lax.rem(xl + dxl, 2) * 2 + lax.rem(core + dc, 2)

    n_z = N_SLAB // 4
    leader = lax.rem(slab, 4) == 3
    zline = (
        (jnp.logical_and(leader, zpos < n_z - 1), slab + 4),
        (jnp.logical_and(leader, zpos > 0), slab - 4),
    )
    across = slab + 2 * core - 1
    paired = jnp.logical_and(across >= 0, across < N_SLAB)
    joint = jnp.logical_and(core == 1, paired)
    lent = jnp.logical_and(core == 0, paired)
    own_first = jnp.logical_not(lent)
    flat = core != xl

    barrier = pltpu.get_barrier_semaphore()
    greeted = [(fro(dx, dy), slab) for dx, dy in PEERS]
    greeted += [(inst, grp(a, b)) for a, b in GROUP]
    expected = len(greeted)
    for who in greeted:
        pl.semaphore_signal(barrier, inc=1, device_id=who, device_id_type=MESH)
    for there, who in zline:
        expected = expected + there.astype(jnp.int32)

        @pl.when(there)
        def _():
            pl.semaphore_signal(barrier, inc=1, device_id=(inst, who), device_id_type=MESH)

    expected = expected + N_INST * paired.astype(jnp.int32)

    @pl.when(paired)
    def _():
        for n in range(N_INST):
            pl.semaphore_signal(barrier, inc=1, device_id=(n, across), device_id_type=MESH)

    loads = [
        pltpu.make_async_copy(src.at[0], dst, in_sem.at[i])
        for i, (src, dst) in enumerate(((vf, a_s), (vu, u_s), (vv, v_s), (vw, w_s), (wet, m_s)))
    ]
    loads.append(pltpu.make_async_copy(sec, s_s, in_sem.at[5]))
    for cp in loads:
        cp.start()
    pl.semaphore_wait(barrier, expected)

    def remote(src, dst, send, recv, where):
        return pltpu.make_async_remote_copy(
            src_ref=src, dst_ref=dst, send_sem=send, recv_sem=recv, device_id=where, device_id_type=MESH
        )

    def strip(n):
        return pl.ds(pl.multiple_of(n * STRIP, STRIP), STRIP)

    def send_out(part, first, count):
        layers = pl.ds(first, count)
        for k, (dx, dy) in enumerate(PEERS):
            peer = to(dx, dy)
            remote(vf.at[0, layers, strip(peer)], got.at[layers, k], p1_send, p1_recv.at[part], (peer, slab)).start()

    n_parts = len(PARTS)
    part_top, part_first = n_parts, n_parts + 1
    everyone = PEERS + ((0, 0),)
    slot = {p: k for k, p in enumerate(everyone)}

    half = pl.ds(pl.multiple_of((1 - xh) * (NY // 2), NY // 2), NY // 2)
    same_half = ((0, 0), (0, 1), (0, 3), (0, 2))

    other_half = tuple((1, k) for k in range(4))

    def lend(pairs):
        for dx, dy in pairs:
            peer = to(dx, dy)
            for q, src in enumerate((vf, vw)):
                remote(src.at[0, 0, strip(peer)], j_got.at[q, slot[(dx, dy)]], j_send, j_recv, (peer, across)).start()

    @pl.when(jnp.logical_and(lent, flat))
    def _():
        for q, src in enumerate((vf, vw)):
            remote(src.at[0, 0, half], relay.at[q], j_send, f_recv, (inst, across)).start()

    @pl.when(jnp.logical_and(lent, jnp.logical_not(flat)))
    def _():
        lend(other_half)

    @pl.when(lent)
    def _():
        lend(same_half)

    send_out(0, *PARTS[0])
    send_out(part_top, TOP, 1)

    def send_w(pairs, n):
        for k, (dx, dy) in enumerate(pairs):
            peer = to(dx, dy)
            remote(vw.at[0, TOP, strip(peer)], w_got.at[3 * n + k], w_send.at[n], w_recv.at[n], (peer, slab)).start()

    @pl.when(joint)
    def _():
        send_w(same_half[1:], 0)

    @pl.when(jnp.logical_and(joint, jnp.logical_not(flat)))
    def _():
        send_w(other_half, 1)

    @pl.when(jnp.logical_not(joint))
    def _():
        w_got[0:3] = jnp.zeros((3, STRIP, NX), F32)
        j_got[...] = jnp.zeros_like(j_got)

    @pl.when(jnp.logical_or(jnp.logical_not(joint), flat))
    def _():
        w_got[3:7] = jnp.zeros((4, STRIP, NX), F32)

    def pass_word(way):
        @pl.when(zline[1 - way][0])
        def _():
            pl.semaphore_wait(word.at[way], 1)

        @pl.when(zline[way][0])
        def _():
            pl.semaphore_signal(word.at[way], inc=1, device_id=(inst, zline[way][1]), device_id_type=MESH)

    def spread():
        for dz in range(1, n_z):
            pltpu.make_async_remote_copy(
                src_ref=tile.at[1], dst_ref=far.at[dz - 1], send_sem=l2_send, recv_sem=l2_recv,
                device_id=(inst, zto(dz)), device_id_type=MESH,
            ).start()

    pass_word(0)

    @pl.when(zpos >= n_z // 2)
    def _():
        pass_word(1)

    for cp in loads:
        cp.wait()

    @pl.when(jnp.logical_and(joint, flat))
    def _():
        pltpu.make_async_copy(relay, relay, f_recv).wait()
        relay_f[...] = flux(w_s[TOP, half], relay[1], a_s[TOP, half], relay[0])
        for k in range(4):
            peer = to(1, k)
            rows = strip(lax.rem(peer, 4))
            for q, src in enumerate((relay.at[0], relay_f)):
                remote(src.at[rows], j_got.at[q, slot[(1, k)]], f_send, j_recv, (peer, slab)).start()

    lane = lax.broadcasted_iota(jnp.int32, (8, NX), 1)
    sub = lax.broadcasted_iota(jnp.int32, (8, NX), 0)
    base = lane // (NX // NSEC)
    total = N_SLAB * CV

    def load_rows(r, sums):
        rows = pl.ds(pl.multiple_of(r * 8, 8), 8)

        def load_layer(v, acc):
            u, vy, w = u_s[v, rows], v_s[v, rows], w_s[v, rows]
            depth = ((slab * CV + v).astype(F32) + 0.5) * (GRAVITY / total)
            pressure = depth + 0.5 * (u * u + vy * vy + w * w)
            load = m_s[v, rows].astype(F32) * a_s[v, rows] * pressure
            rel = s_s[v, rows] - base
            return tuple(a + jnp.where(rel == o, load, 0.0) for a, o in zip(acc, (-1, 0, 1)))

        acc = lax.fori_loop(0, CV, load_layer, (jnp.zeros((8, NX), F32),) * 3)
        lever = ((r * 8 + sub).astype(F32) + 0.5) * (1.0 / NY)
        return tuple(s + a for s, a in zip(sums[:3], acc)) + tuple(s + a * lever for s, a in zip(sums[3:], acc))

    sums = lax.fori_loop(0, NY // 8, load_rows, (jnp.zeros((8, NX), F32),) * 6)
    term = jnp.zeros((16, 128), F32)
    col = lax.broadcasted_iota(jnp.int32, (NX, 128), 0) // (NX // NSEC)
    secs = lax.broadcasted_iota(jnp.int32, (NX, 128), 1)
    for n, o in enumerate((-1, 0, 1)):
        pick = (col + o == secs).astype(F32)
        both = jnp.concatenate([sums[n], sums[3 + n]], axis=0)
        term = term + jnp.dot(both, pick, precision=lax.Precision.HIGHEST, preferred_element_type=F32)
    force = jnp.sum(term[:8], axis=0, keepdims=True)
    moment = jnp.sum(term[8:], axis=0, keepdims=True)
    sub128 = lax.broadcasted_iota(jnp.int32, (8, 128), 0)
    tile[0] = jnp.where(sub128 == 0, force, jnp.where(sub128 == 1, moment, 0.0)) * (2.0 / (CV * NY * NX))
    for k, (a, b) in enumerate(GROUP):
        pltpu.make_async_remote_copy(
            src_ref=tile.at[0], dst_ref=near.at[k], send_sem=l1_send, recv_sem=l1_recv,
            device_id=(inst, grp(a, b)), device_id_type=MESH,
        ).start()

    @pl.when(own_first)
    def _():
        for k, (dx, dy) in enumerate(PEERS):
            peer = to(dx, dy)
            remote(vf.at[0, 0, strip(peer)], got.at[0, k], first_send, p1_recv.at[part_first], (peer, slab)).start()

    for part in range(1, n_parts):
        send_out(part, *PARTS[part])

    inner_layer = TOP - TOP * core
    halo_cps = [
        remote(src.at[0, inner_layer], halo.at[core, q], h_send.at[q], h_recv.at[q], (inst, slab + 1 - 2 * core))
        for q, src in enumerate((vf, vw))
    ]
    for cp in halo_cps:
        cp.start()
    halo[core] = jnp.zeros((2, NY, NX), F32)

    plane[...] = jnp.zeros_like(plane)
    first_lane, last_lane = lane == 0, lane == NX - 1
    first_sub, last_sub = sub == 0, sub == 7

    def one_layer(v, _):
        above = jnp.minimum(v + 1, CV - 1)
        inner = jnp.where(v < CV - 1, 1.0, 0.0)
        prev = None
        for r in range(NY // 8):
            rows = pl.ds(r * 8, 8)
            a, u, s, w = a_s[v, rows], u_s[v, rows], v_s[v, rows], w_s[v, rows]
            top = flux(w, w_s[above, rows], a, a_s[above, rows]) * inner
            d = top - plane[rows]
            plane[rows] = top
            if r < NY // 8 - 1:
                nxt = pl.ds(r * 8 + 8, 8)
                a_n, s_n = pltpu.roll(a_s[v, nxt], 7, 0), pltpu.roll(v_s[v, nxt], 7, 0)
            else:
                a_n = s_n = jnp.zeros((8, NX), F32)
            a_up = jnp.where(last_sub, a_n, pltpu.roll(a, 7, 0))
            s_up = jnp.where(last_sub, s_n, pltpu.roll(s, 7, 0))
            fy = flux(s, s_up, a, a_up)
            fy_roll = pltpu.roll(fy, 1, 0)
            if prev is None:
                low = jnp.minimum(0.5 * s, 0.0) * a
            else:
                low = prev
            d = d + (fy - jnp.where(first_sub, low, fy_roll))
            prev = fy_roll
            a_r = jnp.where(last_lane, 0.0, pltpu.roll(a, NX - 1, 1))
            u_r = jnp.where(last_lane, 0.0, pltpu.roll(u, NX - 1, 1))
            fx = flux(u, u_r, a, a_r)
            left = jnp.minimum(0.5 * u, 0.0) * a
            d = d + (fx - jnp.where(first_lane, left, pltpu.roll(fx, 1, 1)))
            div[v, rows] = d
        return 0

    lax.fori_loop(0, CV, one_layer, 0)

    pltpu.make_async_copy(near, near, l1_recv).wait()
    tile[1] = tile[0] + near[0] + near[1] + near[2]

    @pl.when(jnp.logical_and(leader, zpos >= n_z // 2))
    def _():
        spread()

    sig = [jnp.where(y >= k, 1.0, -1.0) for k in range(4)]
    tau = [jnp.where(y + k < 4, 0.5, -0.5) for k in range(4)]
    mine = strip(inst)

    def circulant(value):
        p = [value(0, k) + value(1, k) for k in range(4)]
        q = [(value(0, k) - value(1, k)) * sig[k] for k in range(4)]
        half_odd, half_even = 0.5 * (p[3] - p[1]), 0.5 * (p[0] - p[2])
        nyq = ((p[0] + p[2]) - (p[1] + p[3])) * (SIGMA / N_INST)
        ps = (half_odd + nyq, -half_even - nyq, nyq - half_odd, half_even - nyq)
        qs = (
            q[2] - ROOT2 * (q[1] + q[3]),
            q[1] - ROOT2 * (q[0] + q[2]),
            q[0] - ROOT2 * (q[1] - q[3]),
            -q[3] - ROOT2 * (q[0] - q[2]),
        )
        out = {}
        for t in range(4):
            qt = qs[t] * tau[t]
            out[(0, t)] = ps[t] + qt
            out[(1, t)] = ps[t] - qt
        return out

    halves = [pl.ds(h * 256, 256) for h in range(2)]

    def arrived(layer, cols):
        def value(e, k):
            if (e, k) == (0, 0):
                return a_s[layer, mine, cols]
            return got[layer, slot[(e, k)], :, cols]

        return value

    def put(layer, cols, out):
        for p, value in out.items():
            if p == (0, 0):
                back[layer, 7, :, cols] = value
            else:
                ret[layer, slot[p], :, cols] = value

    def all_of(ref, sem):
        pltpu.make_async_copy(ref, ref, sem).wait()

    def one_strip(layer, _):
        for cols in halves:
            put(layer, cols, circulant(arrived(layer, cols)))
        return 0

    def send_back(part, first, count, send):
        layers = pl.ds(first, count)
        for k, (dx, dy) in enumerate(PEERS):
            remote(ret.at[layers, k], back.at[layers, k], send, p2_recv.at[part], (to(dx, dy), slab)).start()

    def combine(part, first, count):
        all_of(got.at[pl.ds(first, count)], p1_recv.at[part])
        lax.fori_loop(first, first + count, one_strip, 0)
        send_back(part, first, count, p2_send)

    def combine_top():
        all_of(got.at[TOP], p1_recv.at[part_top])

        @pl.when(joint)
        def _():
            all_of(w_got.at[pl.ds(0, 3)], w_recv.at[0])
            all_of(j_got, j_recv)

        @pl.when(jnp.logical_and(joint, jnp.logical_not(flat)))
        def _():
            all_of(w_got.at[pl.ds(3, 4)], w_recv.at[1])

        use = jnp.where(joint, 1.0, 0.0)
        for cols in halves:
            alpha = arrived(TOP, cols)
            face = {}
            for e, k in everyone:
                n = slot[(e, k)]
                if n == 7:
                    w = w_s[TOP, mine, cols]
                else:
                    w = w_got[3 + k if e else same_half.index((e, k)) - 1, :, cols]
                f = flux(w, j_got[1, n, :, cols], alpha(e, k), j_got[0, n, :, cols])
                if e:
                    f = jnp.where(flat, j_got[1, n, :, cols], f)
                face[(e, (4 - k) % 4)] = use * f
            out = circulant(alpha)
            put(TOP, cols, {p: out[p] + face[p] for p in out})
            out = circulant(lambda e, k: j_got[0, slot[(e, k)], :, cols])
            for p in out:
                j_ret[slot[p], :, cols] = out[p] - face[p]
        send_back(part_top, TOP, 1, p2_send)

        @pl.when(joint)
        def _():
            for k, (dx, dy) in enumerate(everyone):
                remote(j_ret.at[k], back.at[0, k], r_send, p2_recv.at[part_first], (to(dx, dy), across)).start()

    combine(0, *PARTS[0])

    @pl.when(own_first)
    def _():
        all_of(got.at[0], p1_recv.at[part_first])
        one_strip(0, 0)
        send_back(part_first, 0, 1, first_send)

    for part in range(1, n_parts):
        combine(part, *PARTS[part])
    combine_top()

    @pl.when(jnp.logical_and(leader, zpos < n_z // 2))
    def _():
        pass_word(1)
        spread()


    for cp in halo_cps:
        cp.wait()
    use_lo = jnp.where(jnp.logical_or(core == 1, slab == 0), 1.0, 0.0)
    use_hi = jnp.where(jnp.logical_or(core == 0, slab == N_SLAB - 1), 1.0, 0.0)

    def edges(r, _):
        rows = pl.ds(pl.multiple_of(r * 8, 8), 8)
        lo = flux(halo[0, 1, rows], w_s[0, rows], halo[0, 0, rows], a_s[0, rows])
        hi = flux(w_s[TOP, rows], halo[1, 1, rows], a_s[TOP, rows], halo[1, 0, rows])
        div[0, rows] = div[0, rows] - use_lo * lo
        div[TOP, rows] = div[TOP, rows] + use_hi * hi
        return 0

    lax.fori_loop(0, NY // 8, edges, 0)

    home = [strip(fro(dx, dy)) for dx, dy in everyone]

    def finish(layer, _):
        for k, rows in enumerate(home):
            res[0, layer, rows] = div[layer, rows] + back[layer, k]
        return 0

    def finish_part(part, first, count):
        theirs = back.at[pl.ds(first, count), pl.ds(0, 7)]
        all_of(theirs, p2_recv.at[part])
        lax.fori_loop(first, first + count, finish, 0)

    finish_part(0, *PARTS[0])

    @pl.when(leader)
    def _():
        all_of(far, l2_recv)
        whole = tile[1]
        for dz in range(1, n_z):
            whole = whole + far[dz - 1]
        summed[...] = whole
        for p, q in GROUP:
            remote(summed, summed, t_send, t_recv, (inst, grp(p, q))).start()

    for part in range(1, n_parts):
        finish_part(part, *PARTS[part])

    finish_part(part_top, TOP, 1)

    @pl.when(lent)
    def _():
        all_of(back.at[0], p2_recv.at[part_first])

    @pl.when(own_first)
    def _():
        all_of(back.at[0, pl.ds(0, 7)], p2_recv.at[part_first])

    finish(0, 0)

    @pl.when(jnp.logical_not(leader))
    def _():
        all_of(summed, t_recv)

    whole = summed[...]
    lane128 = lax.broadcasted_iota(jnp.int32, (8, 128), 1)
    for e in range(2):
        one = jnp.sum(jnp.where(lane128 == slab * 2 + e, whole, 0.0), axis=1, keepdims=True)
        owned[0, :, e:e + 1] = one[:2]

    all_of(got.at[pl.ds(1, CV - 1)], p1_send)
    all_of(ret.at[pl.ds(1, CV - 1)], p2_send)

    @pl.when(own_first)
    def _():
        all_of(got.at[pl.ds(0, 2)], first_send)

    @pl.when(lent)
    def _():
        all_of(j_got, j_send)

    @pl.when(joint)
    def _():
        all_of(w_got.at[pl.ds(0, 3)], w_send.at[0])
        all_of(j_ret, r_send)

    @pl.when(jnp.logical_and(joint, flat))
    def _():
        all_of(j_ret, f_send)

    @pl.when(jnp.logical_and(joint, jnp.logical_not(flat)))
    def _():
        all_of(w_got.at[pl.ds(3, 4)], w_send.at[1])

    pltpu.make_async_copy(near, near, l1_send).wait()

    @pl.when(leader)
    def _():
        all_of(far, l2_send)
        all_of(near, t_send)


def hand_over(res, owned, res_out, owned_out, sem):
    copies = [
        pltpu.make_async_copy(src, dst, sem.at[n]) for n, (src, dst) in enumerate(((res, res_out), (owned, owned_out)))
    ]
    for cp in copies:
        cp.start()
    for cp in copies:
        cp.wait()


def on_device(*args):
    hbm, vmem = pl.BlockSpec(memory_space=pltpu.HBM), pl.BlockSpec(memory_space=pltpu.VMEM)
    block = (CV, NY, NX)
    dma = pltpu.SemaphoreType.DMA
    made = pl.pallas_call(
        kernel,
        out_shape=(jax.ShapeDtypeStruct((1,) + block, F32), jax.ShapeDtypeStruct((1, 2, 2), F32)),
        in_specs=[hbm] * 6,
        out_specs=(vmem, vmem),
        scratch_shapes=[
            pltpu.VMEM(block, F32), pltpu.VMEM(block, F32), pltpu.VMEM(block, F32), pltpu.VMEM(block, F32),
            pltpu.VMEM(block, jnp.int32), pltpu.VMEM(block, jnp.int32),
            pltpu.VMEM((CV, 7, STRIP, NX), F32),
            pltpu.VMEM((CV, 7, STRIP, NX), F32),
            pltpu.VMEM((CV, 8, STRIP, NX), F32),
            pltpu.VMEM((7, STRIP, NX), F32), pltpu.VMEM((2, 8, STRIP, NX), F32), pltpu.VMEM((8, STRIP, NX), F32),
            pltpu.VMEM((2, NY // 2, NX), F32), pltpu.VMEM((NY // 2, NX), F32),
            pltpu.VMEM(block, F32),
            pltpu.VMEM((NY, NX), F32),
            pltpu.VMEM((2, 2, NY, NX), F32),
            pltpu.VMEM((2, 8, 128), F32), pltpu.VMEM((3, 8, 128), F32), pltpu.VMEM((N_SLAB // 4 - 1, 8, 128), F32),
            pltpu.VMEM((8, 128), F32),
            dma((6,)), dma, dma((len(PARTS) + 2,)), dma, dma((len(PARTS) + 2,)), dma, dma((2,)), dma((2,)), dma, dma, dma, dma, dma,
            dma((2,)), dma((2,)),
            dma, dma, dma, dma, dma, dma, pltpu.SemaphoreType.REGULAR((2,)),
        ],
        compiler_params=pltpu.CompilerParams(
            collective_id=0, has_side_effects=True, vmem_limit_bytes=52 << 20
        ),
        cost_estimate=pl.CostEstimate(flops=20_000_000, bytes_accessed=8 << 20, transcendentals=0),
    )(*args)
    return pl.pallas_call(
        hand_over,
        out_shape=tuple(jax.ShapeDtypeStruct(m.shape, F32) for m in made),
        in_specs=[vmem, vmem],
        out_specs=(hbm, hbm),
        scratch_shapes=[dma((2,))],
        compiler_params=pltpu.CompilerParams(vmem_limit_bytes=1 << 20),
    )(*made)


def solution(mesh):
    placed = (
        P("inst", "slab", None, None),
        P("inst", "slab", None, None),
        P("inst", "slab", None, None),
        P("inst", "slab", None, None),
        P("inst", "slab", None, None),
        P("slab", None, None),
    )
    return jax.shard_map(
        on_device,
        mesh=mesh,
        in_specs=placed,
        out_specs=(P("inst", "slab", None, None), P("inst", None, "slab")),
        check_vma=False,
    )
```

```python
import functools
import math

import jax
import jax.numpy as jnp
from jax import lax
from jax.experimental import pallas as pl
from jax.experimental.pallas import tpu as pltpu
from jax.sharding import PartitionSpec as P

MESH = pl.DeviceIdType.MESH
F32 = jnp.float32

GRAVITY = 4.0
SIGMA = 1.0
ROOT2 = math.sqrt(2.0)

CV, NY, NX = 8, 64, 512
N_INST, N_SLAB = 8, 32
NSEC = 64
STRIP = NY // N_INST
PARTS = ((1, 3), (4, 3))
TOP = CV - 1

PEERS = ((1, 2), (1, 1), (1, 3), (1, 0), (0, 2), (0, 1), (0, 3))
GROUP = ((0, 1), (1, 0), (1, 1))


def flux(speed_lo, speed_hi, lower, upper):
    f = 0.5 * (speed_lo + speed_hi)
    return jnp.maximum(f, 0.0) * lower + jnp.minimum(f, 0.0) * upper


def kernel(vf, vu, vv, vw, wet, sec, res, owned,
           a_s, u_s, v_s, w_s, m_s, s_s, got, ret, back, w_got, j_got, j_ret, relay, relay_f, div, plane, halo, tile, near, far, summed,
           in_sem, p1_send, p1_recv, p2_send, p2_recv, first_send, w_send, w_recv, j_send, j_recv, f_send, f_recv, r_send,
           h_send, h_recv, l1_send, l1_recv, l2_send, l2_recv, t_send, t_recv, word):
    inst = lax.axis_index("inst")
    slab = lax.axis_index("slab")
    xh, y = inst // 4, lax.rem(inst, 4)
    zpos, xl, core = slab // 4, lax.rem(slab // 2, 2), lax.rem(slab, 2)

    def to(dx, dy):
        return lax.rem(xh + dx, 2) * 4 + lax.rem(y + dy, 4)

    def fro(dx, dy):
        return lax.rem(xh + dx, 2) * 4 + lax.rem(y + 4 - dy, 4)

    def zto(dz):
        return lax.rem(zpos + dz, n_z) * 4 + xl * 2 + core

    def grp(dxl, dc):
        return zpos * 4 + lax.rem(xl + dxl, 2) * 2 + lax.rem(core + dc, 2)

    n_z = N_SLAB // 4
    leader = lax.rem(slab, 4) == 3
    zline = (
        (jnp.logical_and(leader, zpos < n_z - 1), slab + 4),
        (jnp.logical_and(leader, zpos > 0), slab - 4),
    )
    across = slab + 2 * core - 1
    paired = jnp.logical_and(across >= 0, across < N_SLAB)
    joint = jnp.logical_and(core == 1, paired)
    lent = jnp.logical_and(core == 0, paired)
    own_first = jnp.logical_not(lent)
    flat = core != xl

    barrier = pltpu.get_barrier_semaphore()
    greeted = [(fro(dx, dy), slab) for dx, dy in PEERS]
    greeted += [(inst, grp(a, b)) for a, b in GROUP]
    expected = len(greeted)
    for who in greeted:
        pl.semaphore_signal(barrier, inc=1, device_id=who, device_id_type=MESH)
    for there, who in zline:
        expected = expected + there.astype(jnp.int32)

        @pl.when(there)
        def _():
            pl.semaphore_signal(barrier, inc=1, device_id=(inst, who), device_id_type=MESH)

    expected = expected + N_INST * paired.astype(jnp.int32)

    @pl.when(paired)
    def _():
        for n in range(N_INST):
            pl.semaphore_signal(barrier, inc=1, device_id=(n, across), device_id_type=MESH)

    loads = [
        pltpu.make_async_copy(src.at[0], dst, in_sem.at[i])
        for i, (src, dst) in enumerate(((vf, a_s), (vu, u_s), (vv, v_s), (vw, w_s), (wet, m_s)))
    ]
    loads.append(pltpu.make_async_copy(sec, s_s, in_sem.at[5]))
    for cp in loads:
        cp.start()
    pl.semaphore_wait(barrier, expected)

    def remote(src, dst, send, recv, where):
        return pltpu.make_async_remote_copy(
            src_ref=src, dst_ref=dst, send_sem=send, recv_sem=recv, device_id=where, device_id_type=MESH
        )

    def strip(n):
        return pl.ds(pl.multiple_of(n * STRIP, STRIP), STRIP)

    def send_out(part, first, count, peers=PEERS):
        layers = pl.ds(first, count)
        for dx, dy in peers:
            peer = to(dx, dy)
            src = vf.at[0, layers, strip(peer)] if part in (0, part_top) else a_s.at[layers, strip(peer)]
            remote(src, got.at[layers, slot[(dx, dy)]], p1_send, p1_recv.at[part], (peer, slab)).start()

    n_parts = len(PARTS)
    part_top, part_first = n_parts, n_parts + 1
    everyone = PEERS + ((0, 0),)
    slot = {p: k for k, p in enumerate(everyone)}

    half = pl.ds(pl.multiple_of((1 - xh) * (NY // 2), NY // 2), NY // 2)
    same_half = ((0, 0), (0, 1), (0, 3), (0, 2))

    other_half = tuple((1, k) for k in range(4))

    def lend(pairs):
        for dx, dy in pairs:
            peer = to(dx, dy)
            for q, src in enumerate((vf, vw)):
                remote(src.at[0, 0, strip(peer)], j_got.at[q, slot[(dx, dy)]], j_send, j_recv, (peer, across)).start()

    @pl.when(jnp.logical_and(lent, flat))
    def _():
        for q, src in enumerate((vf, vw)):
            remote(src.at[0, 0, half], relay.at[q], j_send, f_recv, (inst, across)).start()

    @pl.when(jnp.logical_and(lent, jnp.logical_not(flat)))
    def _():
        lend(other_half)

    @pl.when(lent)
    def _():
        lend(same_half)

    for peers in (PEERS[:4], PEERS[4:]):
        send_out(0, *PARTS[0], peers)
        send_out(part_top, TOP, 1, peers)

    def send_w(pairs, n):
        for k, (dx, dy) in enumerate(pairs):
            peer = to(dx, dy)
            remote(vw.at[0, TOP, strip(peer)], w_got.at[3 * n + k], w_send.at[n], w_recv.at[n], (peer, slab)).start()

    @pl.when(joint)
    def _():
        send_w(same_half[1:], 0)

    @pl.when(jnp.logical_and(joint, jnp.logical_not(flat)))
    def _():
        send_w(other_half, 1)

    @pl.when(jnp.logical_not(joint))
    def _():
        w_got[0:3] = jnp.zeros((3, STRIP, NX), F32)
        j_got[...] = jnp.zeros_like(j_got)

    @pl.when(jnp.logical_or(jnp.logical_not(joint), flat))
    def _():
        w_got[3:7] = jnp.zeros((4, STRIP, NX), F32)

    def pass_word(way):
        @pl.when(zline[1 - way][0])
        def _():
            pl.semaphore_wait(word.at[way], 1)

        @pl.when(zline[way][0])
        def _():
            pl.semaphore_signal(word.at[way], inc=1, device_id=(inst, zline[way][1]), device_id_type=MESH)

    def spread():
        for dz in range(1, n_z):
            pltpu.make_async_remote_copy(
                src_ref=tile.at[1], dst_ref=far.at[dz - 1], send_sem=l2_send, recv_sem=l2_recv,
                device_id=(inst, zto(dz)), device_id_type=MESH,
            ).start()

    pass_word(0)

    @pl.when(zpos >= n_z // 2)
    def _():
        pass_word(1)

    for cp in loads:
        cp.wait()

    @pl.when(jnp.logical_and(joint, flat))
    def _():
        pltpu.make_async_copy(relay, relay, f_recv).wait()
        relay_f[...] = flux(w_s[TOP, half], relay[1], a_s[TOP, half], relay[0])
        for k in range(4):
            peer = to(1, k)
            rows = strip(lax.rem(peer, 4))
            for q, src in enumerate((relay.at[0], relay_f)):
                remote(src.at[rows], j_got.at[q, slot[(1, k)]], f_send, j_recv, (peer, slab)).start()

    lane = lax.broadcasted_iota(jnp.int32, (8, NX), 1)
    sub = lax.broadcasted_iota(jnp.int32, (8, NX), 0)
    base = lane // (NX // NSEC)
    total = N_SLAB * CV

    def load_rows(r, sums):
        rows = pl.ds(pl.multiple_of(r * 8, 8), 8)

        def load_layer(v, acc):
            u, vy, w = u_s[v, rows], v_s[v, rows], w_s[v, rows]
            depth = ((slab * CV + v).astype(F32) + 0.5) * (GRAVITY / total)
            pressure = depth + 0.5 * (u * u + vy * vy + w * w)
            load = m_s[v, rows].astype(F32) * a_s[v, rows] * pressure
            rel = s_s[v, rows] - base
            return tuple(a + jnp.where(rel == o, load, 0.0) for a, o in zip(acc, (-1, 0, 1)))

        acc = lax.fori_loop(0, CV, load_layer, (jnp.zeros((8, NX), F32),) * 3)
        lever = ((r * 8 + sub).astype(F32) + 0.5) * (1.0 / NY)
        return tuple(s + a for s, a in zip(sums[:3], acc)) + tuple(s + a * lever for s, a in zip(sums[3:], acc))

    sums = lax.fori_loop(0, NY // 8, load_rows, (jnp.zeros((8, NX), F32),) * 6)
    term = jnp.zeros((16, 128), F32)
    col = lax.broadcasted_iota(jnp.int32, (NX, 128), 0) // (NX // NSEC)
    secs = lax.broadcasted_iota(jnp.int32, (NX, 128), 1)
    for n, o in enumerate((-1, 0, 1)):
        pick = (col + o == secs).astype(F32)
        both = jnp.concatenate([sums[n], sums[3 + n]], axis=0)
        term = term + jnp.dot(both, pick, precision=lax.Precision.HIGHEST, preferred_element_type=F32)
    force = jnp.sum(term[:8], axis=0, keepdims=True)
    moment = jnp.sum(term[8:], axis=0, keepdims=True)
    sub128 = lax.broadcasted_iota(jnp.int32, (8, 128), 0)
    tile[0] = jnp.where(sub128 == 0, force, jnp.where(sub128 == 1, moment, 0.0)) * (2.0 / (CV * NY * NX))
    for k, (a, b) in enumerate(GROUP):
        pltpu.make_async_remote_copy(
            src_ref=tile.at[0], dst_ref=near.at[k], send_sem=l1_send, recv_sem=l1_recv,
            device_id=(inst, grp(a, b)), device_id_type=MESH,
        ).start()

    @pl.when(own_first)
    def _():
        for k, (dx, dy) in enumerate(PEERS):
            peer = to(dx, dy)
            remote(vf.at[0, 0, strip(peer)], got.at[0, k], first_send, p1_recv.at[part_first], (peer, slab)).start()

    for part in range(1, n_parts):
        send_out(part, *PARTS[part])

    inner_layer = TOP - TOP * core
    halo_cps = [
        remote(src.at[0, inner_layer], halo.at[core, q], h_send.at[q], h_recv.at[q], (inst, slab + 1 - 2 * core))
        for q, src in enumerate((vf, vw))
    ]
    for cp in halo_cps:
        cp.start()
    halo[core] = jnp.zeros((2, NY, NX), F32)

    plane[...] = jnp.zeros_like(plane)
    first_lane, last_lane = lane == 0, lane == NX - 1
    first_sub, last_sub = sub == 0, sub == 7

    def one_layer(v, _):
        above = jnp.minimum(v + 1, CV - 1)
        inner = jnp.where(v < CV - 1, 1.0, 0.0)
        prev = None
        for r in range(NY // 8):
            rows = pl.ds(r * 8, 8)
            a, u, s, w = a_s[v, rows], u_s[v, rows], v_s[v, rows], w_s[v, rows]
            top = flux(w, w_s[above, rows], a, a_s[above, rows]) * inner
            d = top - plane[rows]
            plane[rows] = top
            if r < NY // 8 - 1:
                nxt = pl.ds(r * 8 + 8, 8)
                a_n, s_n = pltpu.roll(a_s[v, nxt], 7, 0), pltpu.roll(v_s[v, nxt], 7, 0)
            else:
                a_n = s_n = jnp.zeros((8, NX), F32)
            a_up = jnp.where(last_sub, a_n, pltpu.roll(a, 7, 0))
            s_up = jnp.where(last_sub, s_n, pltpu.roll(s, 7, 0))
            fy = flux(s, s_up, a, a_up)
            fy_roll = pltpu.roll(fy, 1, 0)
            if prev is None:
                low = jnp.minimum(0.5 * s, 0.0) * a
            else:
                low = prev
            d = d + (fy - jnp.where(first_sub, low, fy_roll))
            prev = fy_roll
            a_r = jnp.where(last_lane, 0.0, pltpu.roll(a, NX - 1, 1))
            u_r = jnp.where(last_lane, 0.0, pltpu.roll(u, NX - 1, 1))
            fx = flux(u, u_r, a, a_r)
            left = jnp.minimum(0.5 * u, 0.0) * a
            d = d + (fx - jnp.where(first_lane, left, pltpu.roll(fx, 1, 1)))
            div[v, rows] = d
        return 0

    lax.fori_loop(0, CV, one_layer, 0)

    pltpu.make_async_copy(near, near, l1_recv).wait()
    tile[1] = tile[0] + near[0] + near[1] + near[2]

    @pl.when(jnp.logical_and(leader, zpos >= n_z // 2))
    def _():
        spread()

    sig = [jnp.where(y >= k, 1.0, -1.0) for k in range(4)]
    tau = [jnp.where(y + k < 4, 0.5, -0.5) for k in range(4)]
    mine = strip(inst)

    def circulant(value):
        p = [value(0, k) + value(1, k) for k in range(4)]
        q = [(value(0, k) - value(1, k)) * sig[k] for k in range(4)]
        half_odd, half_even = 0.5 * (p[3] - p[1]), 0.5 * (p[0] - p[2])
        nyq = ((p[0] + p[2]) - (p[1] + p[3])) * (SIGMA / N_INST)
        ps = (half_odd + nyq, -half_even - nyq, nyq - half_odd, half_even - nyq)
        qs = (
            q[2] - ROOT2 * (q[1] + q[3]),
            q[1] - ROOT2 * (q[0] + q[2]),
            q[0] - ROOT2 * (q[1] - q[3]),
            -q[3] - ROOT2 * (q[0] - q[2]),
        )
        out = {}
        for t in range(4):
            qt = qs[t] * tau[t]
            out[(0, t)] = ps[t] + qt
            out[(1, t)] = ps[t] - qt
        return out

    halves = [pl.ds(h * 256, 256) for h in range(2)]

    def arrived(layer, cols):
        def value(e, k):
            if (e, k) == (0, 0):
                return a_s[layer, mine, cols]
            return got[layer, slot[(e, k)], :, cols]

        return value

    def put(layer, cols, out):
        for p, value in out.items():
            if p == (0, 0):
                back[layer, 7, :, cols] = value
            else:
                ret[layer, slot[p], :, cols] = value

    def all_of(ref, sem):
        pltpu.make_async_copy(ref, ref, sem).wait()

    def one_strip(layer, _):
        for cols in halves:
            put(layer, cols, circulant(arrived(layer, cols)))
        return 0

    def send_back(part, first, count, send):
        layers = pl.ds(first, count)
        for k, (dx, dy) in enumerate(PEERS):
            remote(ret.at[layers, k], back.at[layers, k], send, p2_recv.at[part], (to(dx, dy), slab)).start()

    def combine(part, first, count):
        all_of(got.at[pl.ds(first, count)], p1_recv.at[part])
        lax.fori_loop(first, first + count, one_strip, 0)
        send_back(part, first, count, p2_send)

    def combine_top():
        all_of(got.at[TOP], p1_recv.at[part_top])

        @pl.when(joint)
        def _():
            all_of(w_got.at[pl.ds(0, 3)], w_recv.at[0])
            all_of(j_got, j_recv)

        @pl.when(jnp.logical_and(joint, jnp.logical_not(flat)))
        def _():
            all_of(w_got.at[pl.ds(3, 4)], w_recv.at[1])

        use = jnp.where(joint, 1.0, 0.0)
        for cols in halves:
            alpha = arrived(TOP, cols)
            face = {}
            for e, k in everyone:
                n = slot[(e, k)]
                if n == 7:
                    w = w_s[TOP, mine, cols]
                else:
                    w = w_got[3 + k if e else same_half.index((e, k)) - 1, :, cols]
                f = flux(w, j_got[1, n, :, cols], alpha(e, k), j_got[0, n, :, cols])
                if e:
                    f = jnp.where(flat, j_got[1, n, :, cols], f)
                face[(e, (4 - k) % 4)] = use * f
            out = circulant(alpha)
            put(TOP, cols, {p: out[p] + face[p] for p in out})
            out = circulant(lambda e, k: j_got[0, slot[(e, k)], :, cols])
            for p in out:
                j_ret[slot[p], :, cols] = out[p] - face[p]
        send_back(part_top, TOP, 1, p2_send)

        @pl.when(joint)
        def _():
            for k, (dx, dy) in enumerate(everyone):
                remote(j_ret.at[k], back.at[0, k], r_send, p2_recv.at[part_first], (to(dx, dy), across)).start()

    combine(0, *PARTS[0])

    @pl.when(own_first)
    def _():
        all_of(got.at[0], p1_recv.at[part_first])
        one_strip(0, 0)
        send_back(part_first, 0, 1, first_send)

    for part in range(1, n_parts):
        combine(part, *PARTS[part])
    combine_top()

    @pl.when(jnp.logical_and(leader, zpos < n_z // 2))
    def _():
        pass_word(1)
        spread()


    for cp in halo_cps:
        cp.wait()
    use_lo = jnp.where(jnp.logical_or(core == 1, slab == 0), 1.0, 0.0)
    use_hi = jnp.where(jnp.logical_or(core == 0, slab == N_SLAB - 1), 1.0, 0.0)

    def edges(r, _):
        rows = pl.ds(pl.multiple_of(r * 8, 8), 8)
        lo = flux(halo[0, 1, rows], w_s[0, rows], halo[0, 0, rows], a_s[0, rows])
        hi = flux(w_s[TOP, rows], halo[1, 1, rows], a_s[TOP, rows], halo[1, 0, rows])
        div[0, rows] = div[0, rows] - use_lo * lo
        div[TOP, rows] = div[TOP, rows] + use_hi * hi
        return 0

    lax.fori_loop(0, NY // 8, edges, 0)

    home = [strip(fro(dx, dy)) for dx, dy in everyone]

    def finish(layer, _):
        for k, rows in enumerate(home):
            res[0, layer, rows] = div[layer, rows] + back[layer, k]
        return 0

    def finish_part(part, first, count):
        theirs = back.at[pl.ds(first, count), pl.ds(0, 7)]
        all_of(theirs, p2_recv.at[part])
        lax.fori_loop(first, first + count, finish, 0)

    finish_part(0, *PARTS[0])

    @pl.when(leader)
    def _():
        all_of(far, l2_recv)
        whole = tile[1]
        for dz in range(1, n_z):
            whole = whole + far[dz - 1]
        summed[...] = whole
        for p, q in GROUP:
            remote(summed, summed, t_send, t_recv, (inst, grp(p, q))).start()

    for part in range(1, n_parts):
        finish_part(part, *PARTS[part])

    finish_part(part_top, TOP, 1)

    @pl.when(lent)
    def _():
        all_of(back.at[0], p2_recv.at[part_first])

    @pl.when(own_first)
    def _():
        all_of(back.at[0, pl.ds(0, 7)], p2_recv.at[part_first])

    finish(0, 0)

    @pl.when(jnp.logical_not(leader))
    def _():
        all_of(summed, t_recv)

    whole = summed[...]
    lane128 = lax.broadcasted_iota(jnp.int32, (8, 128), 1)
    for e in range(2):
        one = jnp.sum(jnp.where(lane128 == slab * 2 + e, whole, 0.0), axis=1, keepdims=True)
        owned[0, :, e:e + 1] = one[:2]

    all_of(got.at[pl.ds(1, CV - 1)], p1_send)
    all_of(ret.at[pl.ds(1, CV - 1)], p2_send)

    @pl.when(own_first)
    def _():
        all_of(got.at[pl.ds(0, 2)], first_send)

    @pl.when(lent)
    def _():
        all_of(j_got, j_send)

    @pl.when(joint)
    def _():
        all_of(w_got.at[pl.ds(0, 3)], w_send.at[0])
        all_of(j_ret, r_send)

    @pl.when(jnp.logical_and(joint, flat))
    def _():
        all_of(j_ret, f_send)

    @pl.when(jnp.logical_and(joint, jnp.logical_not(flat)))
    def _():
        all_of(w_got.at[pl.ds(3, 4)], w_send.at[1])

    pltpu.make_async_copy(near, near, l1_send).wait()

    @pl.when(leader)
    def _():
        all_of(far, l2_send)
        all_of(near, t_send)


def hand_over(res, owned, res_out, owned_out, sem):
    copies = [
        pltpu.make_async_copy(src, dst, sem.at[n]) for n, (src, dst) in enumerate(((res, res_out), (owned, owned_out)))
    ]
    for cp in copies:
        cp.start()
    for cp in copies:
        cp.wait()


def on_device(*args):
    hbm, vmem = pl.BlockSpec(memory_space=pltpu.HBM), pl.BlockSpec(memory_space=pltpu.VMEM)
    block = (CV, NY, NX)
    dma = pltpu.SemaphoreType.DMA
    made = pl.pallas_call(
        kernel,
        out_shape=(jax.ShapeDtypeStruct((1,) + block, F32), jax.ShapeDtypeStruct((1, 2, 2), F32)),
        in_specs=[hbm] * 6,
        out_specs=(vmem, vmem),
        scratch_shapes=[
            pltpu.VMEM(block, F32), pltpu.VMEM(block, F32), pltpu.VMEM(block, F32), pltpu.VMEM(block, F32),
            pltpu.VMEM(block, jnp.int32), pltpu.VMEM(block, jnp.int32),
            pltpu.VMEM((CV, 7, STRIP, NX), F32),
            pltpu.VMEM((CV, 7, STRIP, NX), F32),
            pltpu.VMEM((CV, 8, STRIP, NX), F32),
            pltpu.VMEM((7, STRIP, NX), F32), pltpu.VMEM((2, 8, STRIP, NX), F32), pltpu.VMEM((8, STRIP, NX), F32),
            pltpu.VMEM((2, NY // 2, NX), F32), pltpu.VMEM((NY // 2, NX), F32),
            pltpu.VMEM(block, F32),
            pltpu.VMEM((NY, NX), F32),
            pltpu.VMEM((2, 2, NY, NX), F32),
            pltpu.VMEM((2, 8, 128), F32), pltpu.VMEM((3, 8, 128), F32), pltpu.VMEM((N_SLAB // 4 - 1, 8, 128), F32),
            pltpu.VMEM((8, 128), F32),
            dma((6,)), dma, dma((len(PARTS) + 2,)), dma, dma((len(PARTS) + 2,)), dma, dma((2,)), dma((2,)), dma, dma, dma, dma, dma,
            dma((2,)), dma((2,)),
            dma, dma, dma, dma, dma, dma, pltpu.SemaphoreType.REGULAR((2,)),
        ],
        compiler_params=pltpu.CompilerParams(
            collective_id=0, has_side_effects=True, vmem_limit_bytes=52 << 20
        ),
        cost_estimate=pl.CostEstimate(flops=20_000_000, bytes_accessed=8 << 20, transcendentals=0),
    )(*args)
    return pl.pallas_call(
        hand_over,
        out_shape=tuple(jax.ShapeDtypeStruct(m.shape, F32) for m in made),
        in_specs=[vmem, vmem],
        out_specs=(hbm, hbm),
        scratch_shapes=[dma((2,))],
        compiler_params=pltpu.CompilerParams(vmem_limit_bytes=1 << 20),
    )(*made)


def solution(mesh):
    placed = (
        P("inst", "slab", None, None),
        P("inst", "slab", None, None),
        P("inst", "slab", None, None),
        P("inst", "slab", None, None),
        P("inst", "slab", None, None),
        P("slab", None, None),
    )
    return jax.shard_map(
        on_device,
        mesh=mesh,
        in_specs=placed,
        out_specs=(P("inst", "slab", None, None), P("inst", None, "slab")),
        check_vma=False,
    )
```
